512 devices in a mesh: grp: 4 (over y), ctx: 32 (over x_lo, z), tp: 4 (over x_hi, core).
Axes of the slice: x: 4 (x_hi: 2, x_lo: 2; x = x_hi * 2 + x_lo), y: 4, z: 16, core: 2. Of those that a mesh axis runs over, the one named last changes fastest.
Arguments:
- state: float32 [4, 512, 5120], P(None, 'ctx', ('grp', 'tp')), may hold values from -6 to 6
- clean_tokens: bfloat16 [512, 5120], P('ctx', ('grp', 'tp')), may hold values from -6 to 6
- w_query: bfloat16 [5120, 4096], P('ctx', ('grp', 'tp')), may hold values from -0.078125 to 0.078125
- w_key: bfloat16 [5120, 4096], P('ctx', ('grp', 'tp')), may hold values from -0.078125 to 0.078125
- w_value: bfloat16 [5120, 4096], P('ctx', ('grp', 'tp')), may hold values from -0.078125 to 0.078125
- w_out: bfloat16 [4096, 5120], P(('grp', 'tp'), 'ctx'), may hold values from -0.09375 to 0.09375
- cache_keys: bfloat16 [16384, 4096], P('ctx', ('grp', 'tp')), may hold values from -200 to 200
- cache_values: bfloat16 [16384, 4096], P('ctx', ('grp', 'tp')), may hold values from -6 to 6
- norm_gain: float32 [5120], P(('grp', 'tp')), may hold values from 0.25 to 1.75
- mod_gain: float32 [5120], P(('grp', 'tp')), may hold values from -3 to 3
- out_gain: float32 [5120], P(('grp', 'tp')), may hold values from 0.1 to 1.9
- levels: float32 [50], replicated, may hold values from 0.05 to 1
- noise_index: int32 [4], replicated, may hold values from 0 to 47
- placement: int32 [64], P('ctx'), may hold values from 0 to 63, each once
- group_mask: int32 [4, 64], replicated, may hold values 0 or 1
Outputs:
- new_state: float32 [4, 512, 5120], P(None, 'ctx', ('grp', 'tp'))
- new_keys: bfloat16 [512, 4096], P('ctx', ('grp', 'tp'))
- new_values: bfloat16 [512, 4096], P('ctx', ('grp', 'tp'))
The draws below stay inside these ranges and needn't reach their ends.
All inputs are finite; a program needn't handle non-finite values.
Results may differ from the reference program's by a relative error of at most 0.0062.
The reference program's roundings to bfloat16 on the way count: a program that leaves them out, or rounds other values in their place, can miss the bound.
Values may be sent and summed in bfloat16 or wider, within the bound.
No kernel may reach another device: no remote copies, remote signals or barrier semaphores. Data moves between devices by JAX's collectives and lax.ppermute only.
A program may use at most 64 MiB of HBM per device.

```python
import math
import jax
import jax.numpy as jnp
from jax import lax

D = 5120
HEADS = 32
HD = 128
FLIGHT = 4
STEPS = 1
LEVELS = 50
SLOT = 256
GROUP = 512
CACHE = 16384
CACHE_GROUPS = 64


def draw_cache_keys(key, part):
    width = HEADS * HD
    base_key = jax.random.fold_in(jax.random.fold_in(key, 11), 0)
    values = jnp.clip(jax.random.normal(base_key, (CACHE, width), jnp.float32), -6.0, 6.0)
    return values.astype(jnp.bfloat16)


def touch_ends(array, stream_key, least, top_value):
    extent = array.shape
    place = [jax.random.randint(jax.random.fold_in(stream_key, axis), (), 0, extent[axis]) for axis in range(len(extent))]
    array = array.at[tuple(place)].set(least)
    longest = extent.index(max(extent))
    place[longest] = (place[longest] + 1) % extent[longest]
    return array.at[tuple(place)].set(top_value)


def block_levels(rng, extent, cuts, low, top_value):
    def one(position, blocks):
        heights = jax.random.uniform(jax.random.fold_in(jax.random.fold_in(rng, 6), position), (blocks,), jnp.float32, low / len(cuts), top_value / len(cuts))
        return jnp.repeat(jnp.exp(heights), extent[position] // blocks).reshape((-1,) + (1,) * (len(extent) - position - 1))

    gain = one(*cuts[0])
    for cut in cuts[1:]:
        gain = gain * one(*cut)
    return gain


def centred(own_key, extent, scale, limit, cuts=(), kind=jnp.bfloat16):
    array = jax.random.normal(own_key, extent, jnp.float32) * scale
    if len(cuts) > 0:
        array = block_levels(own_key, extent, cuts, -0.22, 0.18) * array
    return jnp.clip(array, min=-limit, max=limit).astype(kind)


def setup_inputs(seed: int = 0) -> dict:
    streams_of = jax.random.split(jax.random.key(seed), 16)
    return {
        "state": centred(streams_of[0], (FLIGHT, GROUP, D), 1.0, 6.0, ((1, 32), (2, 16)), jnp.float32),
        "clean_tokens": centred(streams_of[1], (GROUP, D), 1.0, 6.0, ((0, 32), (1, 16))),
        "w_query": centred(streams_of[2], (D, HEADS * HD), D ** -0.5, 0.078125, ((0, 32), (1, 16))),
        "w_key": centred(streams_of[3], (D, HEADS * HD), D ** -0.5, 0.078125, ((0, 32), (1, 16))),
        "w_value": centred(streams_of[4], (D, HEADS * HD), D ** -0.5, 0.078125, ((0, 32), (1, 16))),
        "w_out": centred(streams_of[5], (HEADS * HD, D), (HEADS * HD) ** -0.5, 0.09375, ((0, 16), (1, 32))),
        "cache_keys": draw_cache_keys(jax.random.fold_in(streams_of[15], 71), 0),
        "cache_values": centred(streams_of[7], (CACHE, HEADS * HD), 1.0, 6.0, ((0, 32), (1, 16))),
        "norm_gain": jnp.clip(1.0 + 0.15 * jax.random.normal(streams_of[8], (D,), jnp.float32), 0.25, 1.75),
        "mod_gain": centred(streams_of[9], (D,), 1.0, 3.0, ((0, 16),), jnp.float32),
        "out_gain": jnp.clip(1.0 + 0.18 * jax.random.normal(streams_of[10], (D,), jnp.float32), 0.1, 1.9),
        "levels": jnp.clip(jax.random.uniform(streams_of[11], (LEVELS,), jnp.float32, 0.05, 1.0), 0.05, 1.0),
        "noise_index": touch_ends(jax.random.randint(streams_of[12], (FLIGHT,), 0, LEVELS - 2), jax.random.fold_in(streams_of[12], 1), 0, (LEVELS - 2) - 1).astype(jnp.int32),
        "placement": jax.random.permutation(streams_of[13], CACHE_GROUPS).astype(jnp.int32),
        "group_mask": touch_ends((jax.random.randint(streams_of[14], (FLIGHT, CACHE_GROUPS), 0, 4) < 3).astype(jnp.int32), jax.random.fold_in(streams_of[14], 1), 0, 1),
    }


epsilon = 1e-06

def normalize(rows, sigma_rows, norm_gain, mod_gain):
    mean_square = lax.optimization_barrier(jnp.mean(rows * rows, axis=1))
    inverse = lax.rsqrt(mean_square + epsilon)
    scaled = rows * inverse[:, None] * norm_gain[None, :] * (1.0 + sigma_rows[:, None] * mod_gain[None, :])
    return scaled.astype(jnp.bfloat16)

def attend(queries, keys, values, seen):
    scale = 1.0 / math.sqrt(HD)

    def one_head(operands):
        query_head, key_head, value_head = operands
        scores = jnp.dot(query_head, key_head.T, preferred_element_type=jnp.float32) * scale
        masked = jnp.where(seen, scores, -jnp.inf)
        peak = lax.optimization_barrier(jnp.max(masked, axis=1, keepdims=True))
        weights = jnp.where(seen, jnp.exp(scores - peak), 0.0).astype(jnp.bfloat16)
        numer = jnp.dot(weights, value_head, preferred_element_type=jnp.float32)
        denom = lax.optimization_barrier(jnp.sum(weights.astype(jnp.float32), axis=1, keepdims=True))
        return (numer / denom).astype(jnp.bfloat16)
    outputs = lax.map(one_head, (queries, keys, values))
    return jnp.transpose(outputs, (1, 0, 2)).reshape(queries.shape[1], HEADS * HD)

def by_heads(matrix):
    return jnp.transpose(matrix.reshape(matrix.shape[0], HEADS, HD), (1, 0, 2))

def reference(state, clean_tokens, w_query, w_key, w_value, w_out, cache_keys, cache_values, norm_gain, mod_gain, out_gain, levels, noise_index, placement, group_mask):
    rows_count = FLIGHT * GROUP
    clean_h = normalize(clean_tokens.astype(jnp.float32), jnp.zeros((GROUP,), jnp.float32), norm_gain, mod_gain)
    new_keys = jnp.dot(clean_h, w_key, preferred_element_type=jnp.float32).astype(jnp.bfloat16)
    new_values = jnp.dot(clean_h, w_value, preferred_element_type=jnp.float32).astype(jnp.bfloat16)
    slot_time = placement[jnp.arange(CACHE, dtype=jnp.int32) // SLOT]
    cache_seen = group_mask[:, slot_time] != 0
    finished_seen = jnp.ones((FLIGHT, GROUP), dtype=bool)
    key_group = jnp.arange(rows_count, dtype=jnp.int32) // GROUP
    own_group = jnp.arange(FLIGHT, dtype=jnp.int32)
    flight_seen = key_group[None, :] <= own_group[:, None]
    seen = jnp.concatenate([cache_seen, finished_seen, flight_seen], axis=1)
    row_seen = jnp.repeat(seen, GROUP, axis=0)
    x = state.reshape(rows_count, D)
    for step in range(STEPS):
        current = levels[noise_index + step]
        following = levels[noise_index + step + 1]
        h = normalize(x, jnp.repeat(current, GROUP), norm_gain, mod_gain)
        q = jnp.dot(h, w_query, preferred_element_type=jnp.float32).astype(jnp.bfloat16)
        k = jnp.dot(h, w_key, preferred_element_type=jnp.float32).astype(jnp.bfloat16)
        v = jnp.dot(h, w_value, preferred_element_type=jnp.float32).astype(jnp.bfloat16)
        all_keys = jnp.concatenate([cache_keys, new_keys, k], axis=0)
        all_values = jnp.concatenate([cache_values, new_values, v], axis=0)
        attention = attend(by_heads(q), by_heads(all_keys), by_heads(all_values), row_seen)
        y = jnp.dot(attention, w_out, preferred_element_type=jnp.float32)
        velocity = y * lax.rsqrt(lax.optimization_barrier(jnp.mean(y * y, axis=1, keepdims=True)) + epsilon) * out_gain[None, :]
        x = x + jnp.repeat(following - current, GROUP)[:, None] * velocity
    return (x.reshape(FLIGHT, GROUP, D), new_keys, new_values)
```

```python
import functools
import math

import jax
import jax.numpy as jnp
from jax import lax
from jax.experimental import pallas as pl
from jax.experimental.pallas import tpu as pltpu
from jax.sharding import Mesh
from jax.sharding import PartitionSpec as P

D = 5120
HD = 128
SLOT = 256
EPSILON = 1e-06
VMEM_LIMIT = 48 * 1024 * 1024

CTX = ("xl", "z")
WIDE = ("y", "xh", "core")
BF16 = jnp.bfloat16
F32 = jnp.float32


def level_lookup(levels, indices):
    table = jnp.arange(levels.shape[0], dtype=jnp.int32)
    picked = (indices[:, None] == table[None, :]).astype(F32)
    return jnp.sum(picked * levels[None, :], axis=1)


def sent_to_all(array, axis):
    devices = lax.axis_size(axis)
    return lax.all_to_all(
        jnp.broadcast_to(array[None], (devices, *array.shape)), axis, 0, 0, tiled=True
    )


def swapped(blocks, axis):
    return lax.all_to_all(blocks, axis, 0, 0, tiled=True)


def by_head(matrix):
    return jnp.stack([matrix[:, :HD], matrix[:, HD:]])


def project_kernel(h_ref, w_ref, q_ref, k_ref, v_ref, vt_ref, acc):
    step = pl.program_id(0)

    @pl.when(step == 0)
    def _():
        acc[...] = jnp.zeros_like(acc)

    total = acc[...]
    for xh in range(2):
        for core in range(2):
            rows = h_ref[core, 0, xh].reshape(160, 320)
            at = 2 * (2 * xh + core)
            weights = w_ref[at : at + 2, 0].reshape(320, 3 * HD)
            total = total + jnp.dot(rows, weights, preferred_element_type=F32)
    acc[...] = total

    @pl.when(step == pl.num_programs(0) - 1)
    def _():
        q_ref[0:64, :] = total[0:64, 0:HD].astype(BF16)
        q_ref[64:128, :] = total[80:144, 0:HD].astype(BF16)
        k_ref[...] = total[:, HD : 2 * HD].astype(BF16)
        v_ref[...] = total[:, 2 * HD :].astype(BF16)
        vt_ref[...] = total[:, 2 * HD :].T.astype(BF16)


def project(features, weights):
    shapes = ((128, HD), (160, HD), (160, HD), (HD, 160))
    return pl.pallas_call(
        project_kernel,
        grid=(4,),
        in_specs=[
            pl.BlockSpec((2, 1, 2, 2, 80, 320), lambda s: (0, s, 0, 0, 0, 0)),
            pl.BlockSpec((8, 1, 160, 3 * HD), lambda s: (s % 2, s // 2, 0, 0)),
        ],
        out_specs=[pl.BlockSpec(shape, lambda s: (0, 0)) for shape in shapes],
        out_shape=[jax.ShapeDtypeStruct(shape, BF16) for shape in shapes],
        scratch_shapes=[pltpu.VMEM((160, 3 * HD), F32)],
        compiler_params=pltpu.CompilerParams(vmem_limit_bytes=VMEM_LIMIT),
        cost_estimate=pl.CostEstimate(
            flops=2 * 160 * D * 384, bytes_accessed=6 * 2**20, transcendentals=0
        ),
    )(features, weights)


def in_three(value):
    high = value.astype(BF16).astype(F32)
    middle = (value - high).astype(BF16).astype(F32)
    return [high, middle, value - high - middle]


def attend_kernel(q_ref, kv_ref, vt_ref, kf_ref, vft_ref, out_ref):
    scale = 1.0 / math.sqrt(HD)
    queries = q_ref[...]
    lanes = queries.shape[0]
    across = (((1,), (1,)), ((), ()))

    def scores(keys):
        return lax.dot_general(keys, queries, across, preferred_element_type=F32) * scale

    parts = []
    for side in range(2):
        seen = kv_ref[side, 1024:1040, :].astype(F32)
        hidden = jnp.where(seen > 0.5, 0.0, -jnp.inf)
        hidden = jnp.concatenate([hidden] * (lanes // HD), axis=1)
        for slot in range(2):
            keys = kv_ref[side, slot * SLOT : (slot + 1) * SLOT, :]
            parts.append(scores(keys) + hidden[slot : slot + 1, :])
    token = lax.broadcasted_iota(jnp.int32, (160, lanes), 0)
    lane = lax.broadcasted_iota(jnp.int32, (160, lanes), 1)
    token = jnp.where(token >= 80, token - 80, token)
    visible = (token >= 64) | ((token >> 4) <= ((lane & 63) >> 4))
    parts.append(jnp.where(visible, scores(kf_ref[...]), -jnp.inf))

    peak = functools.reduce(
        jnp.maximum, [jnp.max(part, axis=0, keepdims=True) for part in parts]
    )
    numer = jnp.zeros((HD, lanes), F32)
    denom = jnp.zeros((1, lanes), F32)
    for i, part in enumerate(parts):
        weights = jnp.exp(part - peak).astype(BF16)
        denom = denom + jnp.sum(weights.astype(F32), axis=0, keepdims=True)
        if i < 4:
            values = vt_ref[i // 2, :, (i % 2) * SLOT : (i % 2 + 1) * SLOT]
        else:
            values = vft_ref[...]
        numer = numer + jnp.dot(values, weights, preferred_element_type=F32)
    mean = (numer / denom).astype(BF16)
    totals = jnp.concatenate(
        [*in_three(peak), *in_three(denom), jnp.zeros((10, lanes), F32)], axis=0
    ).astype(BF16)
    for block in range(lanes // HD):
        at = slice(block * HD, (block + 1) * HD)
        out_ref[block, 0:HD, :] = mean[:, at]
        out_ref[block, HD : HD + 16, :] = totals[:, at]


def attend(queries, kv, values_t, fresh_k, fresh_vt):
    step = 256
    rows = queries.shape[0]

    def whole(array):
        return pl.BlockSpec(array.shape, lambda s: (0,) * array.ndim)

    return pl.pallas_call(
        attend_kernel,
        grid=(rows // step,),
        in_specs=[
            pl.BlockSpec((step, HD), lambda s: (s, 0)),
            whole(kv),
            whole(values_t),
            whole(fresh_k),
            whole(fresh_vt),
        ],
        out_specs=pl.BlockSpec((step // HD, HD + 16, HD), lambda s: (s, 0, 0)),
        out_shape=jax.ShapeDtypeStruct((rows // HD, HD + 16, HD), BF16),
        compiler_params=pltpu.CompilerParams(vmem_limit_bytes=VMEM_LIMIT),
        cost_estimate=pl.CostEstimate(
            flops=4 * rows * 1184 * HD,
            bytes_accessed=3 * 2**20,
            transcendentals=rows * 1184,
        ),
    )(queries, kv, values_t, fresh_k, fresh_vt)


def combine_kernel(in_ref, out_ref):
    totals = in_ref[:, HD : HD + 16, :].astype(F32)
    peak = totals[:, 0, :] + totals[:, 1, :] + totals[:, 2, :]
    denom = totals[:, 3, :] + totals[:, 4, :] + totals[:, 5, :]
    top = jnp.max(peak, axis=0, keepdims=True)
    share = denom * jnp.exp(peak - top)
    share = share / jnp.sum(share, axis=0, keepdims=True)
    mixed = jnp.zeros((HD, HD), F32)
    for i in range(in_ref.shape[0]):
        mixed = mixed + in_ref[i, 0:HD, :].astype(F32) * share[i : i + 1, :]
    out_ref[...] = mixed.T.astype(BF16)


def combine(parts):
    return pl.pallas_call(
        combine_kernel,
        out_shape=jax.ShapeDtypeStruct((HD, HD), BF16),
        compiler_params=pltpu.CompilerParams(vmem_limit_bytes=VMEM_LIMIT),
    )(parts)


def output_kernel(att_ref, w_ref, y_ref):
    attention = jnp.concatenate([att_ref[0], att_ref[1]], axis=1)
    for z in range(16):
        part = jnp.dot(attention, w_ref[z], preferred_element_type=F32)
        for xl in range(2):
            j = 8 * xl + z // 2
            at = 160 * (z % 2)
            y_ref[j % 2, j // 2, :, at : at + 160] = part[:, 160 * xl : 160 * (xl + 1)]


def output_projection(attention, weights):
    return pl.pallas_call(
        output_kernel,
        out_shape=jax.ShapeDtypeStruct((2, 8, 64, 320), F32),
        compiler_params=pltpu.CompilerParams(vmem_limit_bytes=VMEM_LIMIT),
    )(attention, weights)


def local(
    state,
    clean_tokens,
    w_query,
    w_key,
    w_value,
    w_out,
    cache_keys,
    cache_values,
    norm_gain,
    mod_gain,
    out_gain,
    levels,
    noise_index,
    placement,
    group_mask,
):
    flight, ch_dev, width = state.shape
    rows_count = flight * ch_dev

    w_heads = jnp.concatenate([by_head(w) for w in (w_query, w_key, w_value)], axis=2)
    w_heads = swapped(w_heads, "xl")
    w_full = lax.all_gather(w_heads.reshape(320, 3 * HD), "z", axis=0, tiled=True)
    w_full = w_full.reshape(16, 2, 160, 3 * HD)

    current = level_lookup(levels, noise_index)
    following = level_lookup(levels, noise_index + 1)
    rows = jnp.concatenate(
        [state.reshape(rows_count, width), clean_tokens.astype(F32)], axis=0
    )
    sigma_rows = jnp.concatenate(
        [jnp.repeat(current, ch_dev), jnp.zeros((ch_dev,), F32)]
    )
    squares = sent_to_all(jnp.sum(rows * rows, axis=1), WIDE).sum(axis=0)
    inverse = lax.rsqrt(squares / D + EPSILON)
    features = (
        rows
        * inverse[:, None]
        * norm_gain[None, :]
        * (1.0 + sigma_rows[:, None] * mod_gain[None, :])
    ).astype(BF16)
    features = sent_to_all(features, ("y", "xh", "xl"))
    features = sent_to_all(features, "core").reshape(2, 4, 2, 2, 80, width)

    table = jnp.arange(group_mask.shape[1], dtype=jnp.int32)
    held = (placement[:, None] == table[None, :]).astype(jnp.int32)
    seen = jnp.sum(held[None, :, :] * group_mask[:, None, :], axis=2) != 0
    seen = jnp.repeat(seen.T.astype(BF16), ch_dev, axis=1)
    seen = jnp.pad(jnp.concatenate([seen, seen], axis=1), ((0, 14), (0, 0)))
    kv = jnp.concatenate(
        [
            by_head(cache_keys),
            by_head(cache_values),
            jnp.broadcast_to(seen[None], (2, *seen.shape)),
        ],
        axis=1,
    )
    kv = swapped(kv, "xl")
    values_t = jnp.transpose(kv[:, 512:1024], (0, 2, 1))

    q, k, v, vt = project(features, w_full)

    w_out_pair = sent_to_all(w_out, "xl")
    w_out_pair = jnp.concatenate([w_out_pair[0], w_out_pair[1]], axis=1)
    w_out_full = lax.all_gather(w_out_pair, "z", axis=0, tiled=False)

    queries = lax.all_gather(q, "z", axis=0, tiled=True)
    parts = attend(queries, kv, values_t, k, vt)
    parts = swapped(parts, "z")
    attention = combine(parts).reshape(2, rows_count, HD)
    attention = swapped(attention, "xl")

    finished = jnp.stack([k.reshape(2, 80, HD)[:, 64:], v.reshape(2, 80, HD)[:, 64:]], 1)
    finished = swapped(finished, "xl")
    new_keys = jnp.concatenate([finished[0, 0], finished[1, 0]], axis=1)
    new_values = jnp.concatenate([finished[0, 1], finished[1, 1]], axis=1)

    y = output_projection(attention, w_out_full)
    y = swapped(y, "core").sum(axis=0)
    y = swapped(y, ("y", "xh")).sum(axis=0)
    y_squares = sent_to_all(jnp.sum(y * y, axis=1), WIDE).sum(axis=0)
    velocity = y * lax.rsqrt(y_squares / D + EPSILON)[:, None] * out_gain[None, :]
    new_state = state + (following - current)[:, None, None] * velocity.reshape(
        flight, ch_dev, width
    )
    return new_state, new_keys, new_values


def solution(mesh):
    fine = Mesh(mesh.devices.reshape(4, 2, 16, 2, 2), ("y", "xl", "z", "xh", "core"))
    in_specs = (
        P(None, CTX, WIDE),
        P(CTX, WIDE),
        P(CTX, WIDE),
        P(CTX, WIDE),
        P(CTX, WIDE),
        P(WIDE, CTX),
        P(CTX, WIDE),
        P(CTX, WIDE),
        P(WIDE),
        P(WIDE),
        P(WIDE),
        P(),
        P(),
        P(CTX),
        P(),
    )
    out_specs = (P(None, CTX, WIDE), P(CTX, WIDE), P(CTX, WIDE))
    return jax.shard_map(local, mesh=fine, in_specs=in_specs, out_specs=out_specs, check_vma=False)
```

```python
import functools
import math

import jax
import jax.numpy as jnp
from jax import lax
from jax.experimental import pallas as pl
from jax.experimental.pallas import tpu as pltpu
from jax.sharding import Mesh
from jax.sharding import PartitionSpec as P

D = 5120
HD = 128
SLOT = 256
EPSILON = 1e-06
VMEM_LIMIT = 56 * 1024 * 1024

CTX = ("xl", "z")
WIDE = ("y", "xh", "core")
BF16 = jnp.bfloat16
F32 = jnp.float32


def level_lookup(levels, indices):
    table = jnp.arange(levels.shape[0], dtype=jnp.int32)
    picked = (indices[:, None] == table[None, :]).astype(F32)
    return jnp.sum(picked * levels[None, :], axis=1)


def sent_to_all(array, axis):
    devices = lax.axis_size(axis)
    return lax.all_to_all(
        jnp.broadcast_to(array[None], (devices, *array.shape)), axis, 0, 0, tiled=True
    )


def swapped(blocks, axis):
    return lax.all_to_all(blocks, axis, 0, 0, tiled=True)


def by_head(matrix):
    return jnp.stack([matrix[:, :HD], matrix[:, HD:]])


def project_kernel(h_ref, w_ref, q_ref, k_ref, v_ref, vt_ref, acc):
    step = pl.program_id(0)

    @pl.when(step == 0)
    def _():
        acc[...] = jnp.zeros_like(acc)

    total = acc[...]
    for xh in range(2):
        for core in range(2):
            rows = h_ref[core, 0, xh].reshape(160, 320)
            at = 2 * (2 * xh + core)
            weights = w_ref[at : at + 2].reshape(320, 3 * HD)
            total = total + jnp.dot(rows, weights, preferred_element_type=F32)
    acc[...] = total

    @pl.when(step == pl.num_programs(0) - 1)
    def _():
        q_ref[0:64, :] = total[0:64, 0:HD].astype(BF16)
        q_ref[64:128, :] = total[80:144, 0:HD].astype(BF16)
        k_ref[...] = total[:, HD : 2 * HD].astype(BF16)
        v_ref[...] = total[:, 2 * HD :].astype(BF16)
        vt_ref[...] = total[:, 2 * HD :].T.astype(BF16)


def project(features, weights):
    shapes = ((128, HD), (160, HD), (160, HD), (HD, 160))
    return pl.pallas_call(
        project_kernel,
        grid=(4,),
        in_specs=[
            pl.BlockSpec((2, 1, 2, 2, 80, 320), lambda s: (0, s, 0, 0, 0, 0)),
            pl.BlockSpec((8, 160, 3 * HD), lambda s: (s % 2, s // 2, 0)),
        ],
        out_specs=[pl.BlockSpec(shape, lambda s: (0, 0)) for shape in shapes],
        out_shape=[jax.ShapeDtypeStruct(shape, BF16) for shape in shapes],
        scratch_shapes=[pltpu.VMEM((160, 3 * HD), F32)],
        compiler_params=pltpu.CompilerParams(vmem_limit_bytes=VMEM_LIMIT),
        cost_estimate=pl.CostEstimate(
            flops=2 * 160 * D * 384, bytes_accessed=6 * 2**20, transcendentals=0
        ),
    )(features, weights)


def in_three(value):
    high = value.astype(BF16).astype(F32)
    middle = (value - high).astype(BF16).astype(F32)
    return [high, middle, value - high - middle]


def attend_kernel(q_ref, kv_ref, vt_ref, kf_ref, vft_ref, out_ref):
    scale = 1.0 / math.sqrt(HD)
    queries = q_ref[...]
    lanes = queries.shape[0]
    across = (((1,), (1,)), ((), ()))

    def scores(keys):
        return lax.dot_general(keys, queries, across, preferred_element_type=F32) * scale

    parts = []
    for side in range(2):
        seen = kv_ref[side, 1024:1040, :].astype(F32)
        hidden = jnp.where(seen > 0.5, 0.0, -jnp.inf)
        hidden = jnp.concatenate([hidden] * (lanes // HD), axis=1)
        for slot in range(2):
            keys = kv_ref[side, slot * SLOT : (slot + 1) * SLOT, :]
            parts.append(scores(keys) + hidden[slot : slot + 1, :])
    token = lax.broadcasted_iota(jnp.int32, (160, lanes), 0)
    lane = lax.broadcasted_iota(jnp.int32, (160, lanes), 1)
    token = jnp.where(token >= 80, token - 80, token)
    visible = (token >= 64) | ((token >> 4) <= ((lane & 63) >> 4))
    parts.append(jnp.where(visible, scores(kf_ref[...]), -jnp.inf))

    peak = functools.reduce(
        jnp.maximum, [jnp.max(part, axis=0, keepdims=True) for part in parts]
    )
    numer = jnp.zeros((HD, lanes), F32)
    denom = jnp.zeros((1, lanes), F32)
    for i, part in enumerate(parts):
        weights = jnp.exp(part - peak).astype(BF16)
        denom = denom + jnp.sum(weights.astype(F32), axis=0, keepdims=True)
        if i < 4:
            values = vt_ref[i // 2, :, (i % 2) * SLOT : (i % 2 + 1) * SLOT]
        else:
            values = vft_ref[...]
        numer = numer + jnp.dot(values, weights, preferred_element_type=F32)
    mean = (numer / denom).astype(BF16)
    totals = jnp.concatenate(
        [*in_three(peak), *in_three(denom), jnp.zeros((10, lanes), F32)], axis=0
    ).astype(BF16)
    for block in range(lanes // HD):
        at = slice(block * HD, (block + 1) * HD)
        out_ref[block, 0:HD, :] = mean[:, at]
        out_ref[block, HD : HD + 16, :] = totals[:, at]


def attend(queries, kv, values_t, fresh_k, fresh_vt):
    step = 256
    rows = queries.shape[0]

    def whole(array):
        return pl.BlockSpec(array.shape, lambda s: (0,) * array.ndim)

    return pl.pallas_call(
        attend_kernel,
        grid=(rows // step,),
        in_specs=[
            pl.BlockSpec((step, HD), lambda s: (s, 0)),
            whole(kv),
            whole(values_t),
            whole(fresh_k),
            whole(fresh_vt),
        ],
        out_specs=pl.BlockSpec((step // HD, HD + 16, HD), lambda s: (s, 0, 0)),
        out_shape=jax.ShapeDtypeStruct((rows // HD, HD + 16, HD), BF16),
        compiler_params=pltpu.CompilerParams(vmem_limit_bytes=VMEM_LIMIT),
        cost_estimate=pl.CostEstimate(
            flops=4 * rows * 1184 * HD,
            bytes_accessed=3 * 2**20,
            transcendentals=rows * 1184,
        ),
    )(queries, kv, values_t, fresh_k, fresh_vt)


def combine_kernel(in_ref, out_ref):
    totals = in_ref[:, HD : HD + 16, :].astype(F32)
    peak = totals[:, 0, :] + totals[:, 1, :] + totals[:, 2, :]
    denom = totals[:, 3, :] + totals[:, 4, :] + totals[:, 5, :]
    top = jnp.max(peak, axis=0, keepdims=True)
    share = denom * jnp.exp(peak - top)
    share = share / jnp.sum(share, axis=0, keepdims=True)
    mixed = jnp.zeros((HD, HD), F32)
    for i in range(in_ref.shape[0]):
        mixed = mixed + in_ref[i, 0:HD, :].astype(F32) * share[i : i + 1, :]
    out_ref[...] = mixed.T.astype(BF16)


def combine(parts):
    return pl.pallas_call(
        combine_kernel,
        out_shape=jax.ShapeDtypeStruct((HD, HD), BF16),
        compiler_params=pltpu.CompilerParams(vmem_limit_bytes=VMEM_LIMIT),
    )(parts)


def spread_kernel(w_ref, out_ref):
    for m in range(8):
        block = w_ref[2 * m : 2 * m + 2].reshape(320, HD)
        out_ref[2 * m] = block
        out_ref[2 * m + 1] = block


def spread(weights):
    return pl.pallas_call(
        spread_kernel,
        grid=(2,),
        in_specs=[pl.BlockSpec((16, 160, HD), lambda s: (0, s, 3))],
        out_specs=pl.BlockSpec((16, 320, HD), lambda s: (s, 0, 0)),
        out_shape=jax.ShapeDtypeStruct((32, 320, HD), BF16),
        compiler_params=pltpu.CompilerParams(vmem_limit_bytes=VMEM_LIMIT),
        cost_estimate=pl.CostEstimate(flops=0, bytes_accessed=4 * 2**20, transcendentals=0),
    )(weights)


def output_kernel(att_ref, w_ref, y_ref):
    total = jnp.zeros(y_ref.shape, F32)
    for i in range(16):
        attention = jnp.concatenate([att_ref[2 * i], att_ref[2 * i + 1]], axis=1)
        weights = jnp.concatenate([w_ref[2 * i], w_ref[2 * i + 1]], axis=1)
        total = total + lax.dot_general(
            attention, weights, (((1,), (1,)), ((), ())), preferred_element_type=F32
        )
    y_ref[...] = total


def output_projection(attention, weights):
    return pl.pallas_call(
        output_kernel,
        out_shape=jax.ShapeDtypeStruct((64, 320), F32),
        compiler_params=pltpu.CompilerParams(vmem_limit_bytes=VMEM_LIMIT),
    )(attention, weights)


def local(
    state,
    clean_tokens,
    w_query,
    w_key,
    w_value,
    w_out,
    cache_keys,
    cache_values,
    norm_gain,
    mod_gain,
    out_gain,
    levels,
    noise_index,
    placement,
    group_mask,
):
    flight, ch_dev, width = state.shape
    rows_count = flight * ch_dev

    parts = [by_head(w) for w in (w_query, w_key, w_value)]
    parts.append(jnp.transpose(w_out.reshape(2, HD, 160), (0, 2, 1)))
    shard = swapped(jnp.concatenate(parts, axis=2), "xl").reshape(320, 4 * HD)
    w_full = lax.all_gather(shard, "z", axis=0, tiled=False)

    current = level_lookup(levels, noise_index)
    following = level_lookup(levels, noise_index + 1)
    rows = jnp.concatenate(
        [state.reshape(rows_count, width), clean_tokens.astype(F32)], axis=0
    )
    sigma_rows = jnp.concatenate(
        [jnp.repeat(current, ch_dev), jnp.zeros((ch_dev,), F32)]
    )
    squares = sent_to_all(jnp.sum(rows * rows, axis=1), WIDE).sum(axis=0)
    inverse = lax.rsqrt(squares / D + EPSILON)
    features = (
        rows
        * inverse[:, None]
        * norm_gain[None, :]
        * (1.0 + sigma_rows[:, None] * mod_gain[None, :])
    ).astype(BF16)
    features = sent_to_all(features, ("y", "xh", "xl"))
    features = sent_to_all(features, "core").reshape(2, 4, 2, 2, 80, width)

    table = jnp.arange(group_mask.shape[1], dtype=jnp.int32)
    held = (placement[:, None] == table[None, :]).astype(jnp.int32)
    seen = jnp.sum(held[None, :, :] * group_mask[:, None, :], axis=2) != 0
    seen = jnp.repeat(seen.T.astype(BF16), ch_dev, axis=1)
    seen = jnp.pad(jnp.concatenate([seen, seen], axis=1), ((0, 14), (0, 0)))
    kv = jnp.concatenate(
        [
            by_head(cache_keys),
            by_head(cache_values),
            jnp.broadcast_to(seen[None], (2, *seen.shape)),
        ],
        axis=1,
    )
    kv = swapped(kv, "xl")
    values_t = jnp.transpose(kv[:, 512:1024], (0, 2, 1))

    w_full, values_t = lax.optimization_barrier((w_full, values_t))
    q, k, v, vt = project(features, w_full)

    w_out_blocks = spread(w_full)
    q, w_out_blocks = lax.optimization_barrier((q, w_out_blocks))
    w_out_full = swapped(w_out_blocks, (*WIDE, "xl"))

    queries = lax.all_gather(q, "z", axis=0, tiled=True)
    parts = attend(queries, kv, values_t, k, vt)
    parts, w_out_full = lax.optimization_barrier((parts, w_out_full))
    parts = swapped(parts, "z")
    attention = combine(parts).reshape(1, 2, rows_count, HD)
    attention = jnp.broadcast_to(attention, (16, 2, rows_count, HD))
    attention = swapped(attention.reshape(32, rows_count, HD), (*WIDE, "xl"))

    finished = jnp.stack([k.reshape(2, 80, HD)[:, 64:], v.reshape(2, 80, HD)[:, 64:]], 1)
    finished = swapped(finished, "xl")
    new_keys = jnp.concatenate([finished[0, 0], finished[1, 0]], axis=1)
    new_values = jnp.concatenate([finished[0, 1], finished[1, 1]], axis=1)

    y = output_projection(attention, w_out_full)
    y_squares = sent_to_all(jnp.sum(y * y, axis=1), WIDE).sum(axis=0)
    velocity = y * lax.rsqrt(y_squares / D + EPSILON)[:, None] * out_gain[None, :]
    new_state = state + (following - current)[:, None, None] * velocity.reshape(
        flight, ch_dev, width
    )
    return new_state, new_keys, new_values


def solution(mesh):
    fine = Mesh(mesh.devices.reshape(4, 2, 16, 2, 2), ("y", "xl", "z", "xh", "core"))
    in_specs = (
        P(None, CTX, WIDE),
        P(CTX, WIDE),
        P(CTX, WIDE),
        P(CTX, WIDE),
        P(CTX, WIDE),
        P(WIDE, CTX),
        P(CTX, WIDE),
        P(CTX, WIDE),
        P(WIDE),
        P(WIDE),
        P(WIDE),
        P(),
        P(),
        P(CTX),
        P(),
    )
    out_specs = (P(None, CTX, WIDE), P(CTX, WIDE), P(CTX, WIDE))
    return jax.shard_map(local, mesh=fine, in_specs=in_specs, out_specs=out_specs, check_vma=False)
```

```python
import functools
import math

import jax
import jax.numpy as jnp
from jax import lax
from jax.experimental import pallas as pl
from jax.experimental.pallas import tpu as pltpu
from jax.sharding import Mesh
from jax.sharding import PartitionSpec as P

D = 5120
HD = 128
SLOT = 256
EPSILON = 1e-06
VMEM_LIMIT = 56 * 1024 * 1024

CTX = ("xl", "z")
WIDE = ("y", "xh", "core")
BF16 = jnp.bfloat16
F32 = jnp.float32


def level_lookup(levels, indices):
    table = jnp.arange(levels.shape[0], dtype=jnp.int32)
    picked = (indices[:, None] == table[None, :]).astype(F32)
    return jnp.sum(picked * levels[None, :], axis=1)


def sent_to_all(array, axis):
    devices = lax.axis_size(axis)
    return lax.all_to_all(
        jnp.broadcast_to(array[None], (devices, *array.shape)), axis, 0, 0, tiled=True
    )


def swapped(blocks, axis):
    return lax.all_to_all(blocks, axis, 0, 0, tiled=True)


def by_head(matrix):
    return jnp.stack([matrix[:, :HD], matrix[:, HD:]])


def project_kernel(h_ref, w_ref, out_ref, acc):
    step = pl.program_id(0)

    @pl.when(step == 0)
    def _():
        acc[...] = jnp.zeros_like(acc)

    total = acc[...]
    for xh in range(2):
        for core in range(2):
            rows = h_ref[core, 0, xh].reshape(160, 320)
            at = 2 * (2 * xh + core)
            weights = w_ref[at : at + 2].reshape(320, 3 * HD)
            total = total + jnp.dot(rows, weights, preferred_element_type=F32)
    acc[...] = total

    @pl.when(step == pl.num_programs(0) - 1)
    def _():
        out_ref[0:64, :] = total[0:64, 0:HD].astype(BF16)
        out_ref[64:128, :] = total[80:144, 0:HD].astype(BF16)
        out_ref[128:288, :] = total[:, HD : 2 * HD].astype(BF16)
        out_ref[288:448, :] = total[:, 2 * HD :].astype(BF16)


def project(features, weights):
    return pl.pallas_call(
        project_kernel,
        grid=(4,),
        in_specs=[
            pl.BlockSpec((2, 1, 2, 2, 80, 320), lambda s: (0, s, 0, 0, 0, 0)),
            pl.BlockSpec((8, 160, 3 * HD), lambda s: (s % 2, s // 2, 0)),
        ],
        out_specs=pl.BlockSpec((448, HD), lambda s: (0, 0)),
        out_shape=jax.ShapeDtypeStruct((448, HD), BF16),
        scratch_shapes=[pltpu.VMEM((160, 3 * HD), F32)],
        compiler_params=pltpu.CompilerParams(vmem_limit_bytes=VMEM_LIMIT),
        cost_estimate=pl.CostEstimate(
            flops=2 * 160 * D * 384, bytes_accessed=6 * 2**20, transcendentals=0
        ),
    )(features, weights)


def in_three(value):
    high = value.astype(BF16).astype(F32)
    middle = (value - high).astype(BF16).astype(F32)
    return [high, middle, value - high - middle]


def attend_kernel(q_ref, kv_ref, vt_ref, new_ref, out_ref, vft_ref):
    @pl.when(pl.program_id(0) == 0)
    def _():
        vft_ref[...] = new_ref[288:448, :].astype(F32).T.astype(BF16)

    scale = 1.0 / math.sqrt(HD)
    queries = q_ref[...]
    lanes = queries.shape[0]
    across = (((1,), (1,)), ((), ()))

    def scores(keys):
        return lax.dot_general(keys, queries, across, preferred_element_type=F32) * scale

    parts = []
    for side in range(2):
        seen = kv_ref[side, 1024:1040, :].astype(F32)
        hidden = jnp.where(seen > 0.5, 0.0, -jnp.inf)
        hidden = jnp.concatenate([hidden] * (lanes // HD), axis=1)
        for slot in range(2):
            keys = kv_ref[side, slot * SLOT : (slot + 1) * SLOT, :]
            parts.append(scores(keys) + hidden[slot : slot + 1, :])
    token = lax.broadcasted_iota(jnp.int32, (160, lanes), 0)
    lane = lax.broadcasted_iota(jnp.int32, (160, lanes), 1)
    token = jnp.where(token >= 80, token - 80, token)
    visible = (token >= 64) | ((token >> 4) <= ((lane & 63) >> 4))
    parts.append(jnp.where(visible, scores(new_ref[128:288, :]), -jnp.inf))

    peak = functools.reduce(
        jnp.maximum, [jnp.max(part, axis=0, keepdims=True) for part in parts]
    )
    numer = jnp.zeros((HD, lanes), F32)
    denom = jnp.zeros((1, lanes), F32)
    for i, part in enumerate(parts):
        weights = jnp.exp(part - peak).astype(BF16)
        denom = denom + jnp.sum(weights.astype(F32), axis=0, keepdims=True)
        if i < 4:
            values = vt_ref[i // 2, :, (i % 2) * SLOT : (i % 2 + 1) * SLOT]
        else:
            values = vft_ref[...]
        numer = numer + jnp.dot(values, weights, preferred_element_type=F32)
    mean = (numer / denom).astype(BF16)
    totals = jnp.concatenate(
        [*in_three(peak), *in_three(denom), jnp.zeros((10, lanes), F32)], axis=0
    ).astype(BF16)
    for block in range(lanes // HD):
        at = slice(block * HD, (block + 1) * HD)
        out_ref[block, 0:HD, :] = mean[:, at]
        out_ref[block, HD : HD + 16, :] = totals[:, at]


def attend(queries, kv, values_t, fresh):
    step = 256
    rows = queries.shape[0]

    def whole(array):
        return pl.BlockSpec(array.shape, lambda s: (0,) * array.ndim)

    return pl.pallas_call(
        attend_kernel,
        grid=(rows // step,),
        in_specs=[
            pl.BlockSpec((step, HD), lambda s: (s, 0)),
            whole(kv),
            whole(values_t),
            whole(fresh),
        ],
        out_specs=pl.BlockSpec((step // HD, HD + 16, HD), lambda s: (s, 0, 0)),
        out_shape=jax.ShapeDtypeStruct((rows // HD, HD + 16, HD), BF16),
        scratch_shapes=[pltpu.VMEM((HD, 160), BF16)],
        compiler_params=pltpu.CompilerParams(vmem_limit_bytes=VMEM_LIMIT),
        cost_estimate=pl.CostEstimate(
            flops=4 * rows * 1184 * HD,
            bytes_accessed=3 * 2**20,
            transcendentals=rows * 1184,
        ),
    )(queries, kv, values_t, fresh)


def combine_kernel(in_ref, out_ref):
    totals = in_ref[:, HD : HD + 16, :].astype(F32)
    peak = totals[:, 0, :] + totals[:, 1, :] + totals[:, 2, :]
    denom = totals[:, 3, :] + totals[:, 4, :] + totals[:, 5, :]
    top = jnp.max(peak, axis=0, keepdims=True)
    share = denom * jnp.exp(peak - top)
    share = share / jnp.sum(share, axis=0, keepdims=True)
    mixed = jnp.zeros((HD, HD), F32)
    for i in range(in_ref.shape[0]):
        mixed = mixed + in_ref[i, 0:HD, :].astype(F32) * share[i : i + 1, :]
    out_ref[...] = mixed.T.astype(BF16)


def combine(parts):
    return pl.pallas_call(
        combine_kernel,
        out_shape=jax.ShapeDtypeStruct((HD, HD), BF16),
        compiler_params=pltpu.CompilerParams(vmem_limit_bytes=VMEM_LIMIT),
    )(parts)


def output_kernel(att_ref, w_ref, y_ref, square_ref):
    total = jnp.zeros((320, 64), F32)
    for i in range(16):
        attention = jnp.concatenate([att_ref[2 * i], att_ref[2 * i + 1]], axis=1)
        total = total + lax.dot_general(
            w_ref[i], attention, (((1,), (1,)), ((), ())), preferred_element_type=F32
        )
    y_ref[...] = total.T
    squares = jnp.sum(total * total, axis=0, keepdims=True)
    for i in range(16):
        square_ref[i] = squares


def output_projection(attention, weights):
    return pl.pallas_call(
        output_kernel,
        out_shape=(
            jax.ShapeDtypeStruct((64, 320), F32),
            jax.ShapeDtypeStruct((16, 1, 64), F32),
        ),
        compiler_params=pltpu.CompilerParams(vmem_limit_bytes=VMEM_LIMIT),
    )(attention, weights)


def turned(array):
    def device(g, z):
        return (g // 4 * 16 + z) * 4 + g % 4

    pairs = [(device(g, c), device(c, g)) for g in range(16) for c in range(16)]
    return lax.ppermute(array, ("y", "z", "xh", "core"), pairs)


def to_owners(array):
    def device(g, xl, z):
        return ((g // 4 * 2 + xl) * 16 + z) * 4 + g % 4

    pairs = [
        (device(g, c // 16, c % 16), device(c // 2, c % 2, g))
        for g in range(16)
        for c in range(32)
    ]
    return lax.ppermute(array, ("y", "xl", "z", "xh", "core"), pairs)


def local(
    state,
    clean_tokens,
    w_query,
    w_key,
    w_value,
    w_out,
    cache_keys,
    cache_values,
    norm_gain,
    mod_gain,
    out_gain,
    levels,
    noise_index,
    placement,
    group_mask,
):
    flight, ch_dev, width = state.shape
    rows_count = flight * ch_dev

    shard = jnp.concatenate([by_head(w) for w in (w_query, w_key, w_value)], axis=2)
    shard = swapped(shard, "xl").reshape(320, 3 * HD)
    w_full = lax.all_gather(shard, "z", axis=0, tiled=False)
    w_out_block = to_owners(w_out.T)

    current = level_lookup(levels, noise_index)
    following = level_lookup(levels, noise_index + 1)
    rows = jnp.concatenate(
        [state.reshape(rows_count, width), clean_tokens.astype(F32)], axis=0
    )
    sigma_rows = jnp.concatenate(
        [jnp.repeat(current, ch_dev), jnp.zeros((ch_dev,), F32)]
    )
    squares = sent_to_all(jnp.sum(rows * rows, axis=1), WIDE).sum(axis=0)
    inverse = lax.rsqrt(squares / D + EPSILON)
    features = (
        rows
        * inverse[:, None]
        * norm_gain[None, :]
        * (1.0 + sigma_rows[:, None] * mod_gain[None, :])
    ).astype(BF16)
    features = sent_to_all(features, ("y", "xh", "xl"))
    features = sent_to_all(features, "core").reshape(2, 4, 2, 2, 80, width)

    table = jnp.arange(group_mask.shape[1], dtype=jnp.int32)
    held = (placement[:, None] == table[None, :]).astype(jnp.int32)
    seen = jnp.sum(held[None, :, :] * group_mask[:, None, :], axis=2) != 0
    seen = jnp.repeat(seen.T.astype(BF16), ch_dev, axis=1)
    seen = jnp.pad(jnp.concatenate([seen, seen], axis=1), ((0, 14), (0, 0)))
    kv = jnp.concatenate(
        [
            by_head(cache_keys),
            by_head(cache_values),
            jnp.broadcast_to(seen[None], (2, *seen.shape)),
        ],
        axis=1,
    )
    kv = turned(swapped(kv, "xl"))
    values_t = jnp.transpose(kv[:, 512:1024], (0, 2, 1))

    w_out_block = sent_to_all(w_out_block, "xl").reshape(320, 2 * HD)
    w_out_full = lax.all_gather(w_out_block, "z", axis=0, tiled=False)

    w_full, values_t = lax.optimization_barrier((w_full, values_t))
    new = project(features, w_full)

    fresh = turned(new)
    queries = sent_to_all(fresh[:HD], WIDE).reshape(-1, HD)
    parts = swapped(attend(queries, kv, values_t, fresh), WIDE)
    attention = turned(combine(parts)).reshape(1, 2, rows_count, HD)
    attention = jnp.broadcast_to(attention, (16, 2, rows_count, HD))
    attention = swapped(attention.reshape(32, rows_count, HD), (*WIDE, "xl"))

    finished = new[128:].reshape(2, 2, 80, HD)[:, :, 64:]
    side = lax.axis_index("xl")
    mine = jnp.where(side == 0, finished[:, 0], finished[:, 1])
    other = jnp.where(side == 0, finished[:, 1], finished[:, 0])
    other = lax.ppermute(other, "xl", [(0, 1), (1, 0)])
    finished = jnp.where(
        side == 0,
        jnp.concatenate([mine, other], axis=2),
        jnp.concatenate([other, mine], axis=2),
    )
    new_keys, new_values = finished[0], finished[1]

    y, y_squares = output_projection(attention, w_out_full)
    y_squares = swapped(y_squares, WIDE).sum(axis=(0, 1))
    velocity = y * lax.rsqrt(y_squares / D + EPSILON)[:, None] * out_gain[None, :]
    new_state = state + (following - current)[:, None, None] * velocity.reshape(
        flight, ch_dev, width
    )
    return new_state, new_keys, new_values


def solution(mesh):
    fine = Mesh(mesh.devices.reshape(4, 2, 16, 2, 2), ("y", "xl", "z", "xh", "core"))
    in_specs = (
        P(None, CTX, WIDE),
        P(CTX, WIDE),
        P(CTX, WIDE),
        P(CTX, WIDE),
        P(CTX, WIDE),
        P(WIDE, CTX),
        P(CTX, WIDE),
        P(CTX, WIDE),
        P(WIDE),
        P(WIDE),
        P(WIDE),
        P(),
        P(),
        P(CTX),
        P(),
    )
    out_specs = (P(None, CTX, WIDE), P(CTX, WIDE), P(CTX, WIDE))
    return jax.shard_map(local, mesh=fine, in_specs=in_specs, out_specs=out_specs, check_vma=False)
```

```python
import functools
import math

import jax
import jax.numpy as jnp
from jax import lax
from jax.experimental import pallas as pl
from jax.experimental.pallas import tpu as pltpu
from jax.sharding import Mesh
from jax.sharding import PartitionSpec as P

D = 5120
HD = 128
SLOT = 256
EPSILON = 1e-06
VMEM_LIMIT = 56 * 1024 * 1024

CTX = ("xl", "z")
WIDE = ("y", "xh", "core")
BF16 = jnp.bfloat16
F32 = jnp.float32


def level_lookup(levels, indices):
    table = jnp.arange(levels.shape[0], dtype=jnp.int32)
    picked = (indices[:, None] == table[None, :]).astype(F32)
    return jnp.sum(picked * levels[None, :], axis=1)


def sent_to_all(array, axis):
    devices = lax.axis_size(axis)
    return lax.all_to_all(
        jnp.broadcast_to(array[None], (devices, *array.shape)), axis, 0, 0, tiled=True
    )


def swapped(blocks, axis):
    return lax.all_to_all(blocks, axis, 0, 0, tiled=True)


def by_head(matrix):
    return jnp.stack([matrix[:, :HD], matrix[:, HD:]])


def project_kernel(h_ref, w_ref, out_ref, acc):
    step = pl.program_id(0)

    @pl.when(step == 0)
    def _():
        acc[...] = jnp.zeros_like(acc)

    total = acc[...]
    width = acc.shape[1]
    for xh in range(2):
        for core in range(2):
            rows = h_ref[core, 0, xh].reshape(160, 320)
            at = 2 * (2 * xh + core)
            weights = w_ref[at : at + 2].reshape(320, width)
            total = total + jnp.dot(rows, weights, preferred_element_type=F32)
    acc[...] = total

    @pl.when(step == pl.num_programs(0) - 1)
    def _():
        if width == HD:
            for xl in range(2):
                rows = total[80 * xl : 80 * xl + 64].astype(BF16)
                for i in range(8):
                    out_ref[2 * i + xl] = rows
        else:
            out_ref[0:160, :] = total[:, 0:HD].astype(BF16)
            out_ref[160:320, :] = total[:, HD:].astype(BF16)


def project(features, weights, block, width, shape):
    return pl.pallas_call(
        project_kernel,
        grid=(4,),
        in_specs=[
            pl.BlockSpec((2, 1, 2, 2, 80, 320), lambda s: (0, s, 0, 0, 0, 0)),
            pl.BlockSpec((8, 160, width), lambda s: (s % 2, s // 2, block)),
        ],
        out_specs=pl.BlockSpec(shape, lambda s: (0,) * len(shape)),
        out_shape=jax.ShapeDtypeStruct(shape, BF16),
        scratch_shapes=[pltpu.VMEM((160, width), F32)],
        compiler_params=pltpu.CompilerParams(vmem_limit_bytes=VMEM_LIMIT),
        cost_estimate=pl.CostEstimate(
            flops=2 * 160 * D * width, bytes_accessed=4 * 2**20, transcendentals=0
        ),
    )(features, weights)


def in_three(value):
    high = value.astype(BF16).astype(F32)
    middle = (value - high).astype(BF16).astype(F32)
    return [high, middle, value - high - middle]


def attend_kernel(q_ref, own_ref, other_ref, own_vt_ref, other_vt_ref, own_new, other_new, out_ref, fresh_vt):
    @pl.when(pl.program_id(0) == 0)
    def _():
        for i, new in enumerate((own_new, other_new)):
            fresh_vt[i] = new[160:320, :].astype(F32).T.astype(BF16)

    scale = 1.0 / math.sqrt(HD)
    queries = q_ref[...]
    lanes = queries.shape[0]
    across = (((1,), (1,)), ((), ()))

    def scores(keys):
        return lax.dot_general(keys, queries, across, preferred_element_type=F32) * scale

    token = lax.broadcasted_iota(jnp.int32, (160, lanes), 0)
    lane = lax.broadcasted_iota(jnp.int32, (160, lanes), 1)
    token = jnp.where(token >= 80, token - 80, token)
    visible = (token >= 64) | ((token >> 4) <= ((lane & 63) >> 4))

    parts, values = [], []
    for i, (kv_ref, vt_ref, new) in enumerate(
        ((own_ref, own_vt_ref, own_new), (other_ref, other_vt_ref, other_new))
    ):
        for side in range(2):
            seen = kv_ref[side, 1024:1040, :].astype(F32)
            hidden = jnp.where(seen > 0.5, 0.0, -jnp.inf)
            hidden = jnp.concatenate([hidden] * (lanes // HD), axis=1)
            for slot in range(2):
                at = slice(slot * SLOT, (slot + 1) * SLOT)
                parts.append(scores(kv_ref[side, at, :]) + hidden[slot : slot + 1, :])
                values.append(vt_ref[side, :, at])
        parts.append(jnp.where(visible, scores(new[0:160, :]), -jnp.inf))
        values.append(fresh_vt[i])

    peak = functools.reduce(
        jnp.maximum, [jnp.max(part, axis=0, keepdims=True) for part in parts]
    )
    numer = jnp.zeros((HD, lanes), F32)
    denom = jnp.zeros((1, lanes), F32)
    for part, value in zip(parts, values):
        weights = jnp.exp(part - peak).astype(BF16)
        denom = denom + jnp.sum(weights.astype(F32), axis=0, keepdims=True)
        numer = numer + jnp.dot(value, weights, preferred_element_type=F32)
    mean = (numer / denom).T.astype(BF16)
    totals = jnp.concatenate(
        [*in_three(peak), *in_three(denom), jnp.zeros((10, lanes), F32)], axis=0
    )
    for block in range(lanes // 64):
        at = slice(block * 64, (block + 1) * 64)
        out_ref[block, 0:64, :] = mean[at, :]
        out_ref[block, 64:80, :] = jnp.concatenate(
            [totals[:, at], totals[:, at]], axis=1
        ).astype(BF16)


def attend(queries, kv, values_t, fresh):
    step = 256
    rows = queries.shape[0]
    arrays = (*kv, *values_t, *fresh)

    def whole(array):
        return pl.BlockSpec(array.shape, lambda s: (0,) * array.ndim)

    return pl.pallas_call(
        attend_kernel,
        grid=(rows // step,),
        in_specs=[
            pl.BlockSpec((step, HD), lambda s: (s, 0)),
            *[whole(array) for array in arrays],
        ],
        out_specs=pl.BlockSpec((step // 64, 80, HD), lambda s: (s, 0, 0)),
        out_shape=jax.ShapeDtypeStruct((rows // 64, 80, HD), BF16),
        scratch_shapes=[pltpu.VMEM((2, HD, 160), BF16)],
        compiler_params=pltpu.CompilerParams(vmem_limit_bytes=VMEM_LIMIT),
        cost_estimate=pl.CostEstimate(
            flops=4 * rows * 2368 * HD,
            bytes_accessed=3 * 2**20,
            transcendentals=rows * 2368,
        ),
    )(queries, *arrays)


def combine_kernel(in_ref, out_ref):
    count = in_ref.shape[0]
    totals = in_ref[:, 64:80, :].astype(F32)
    peak = totals[:, 0, :] + totals[:, 1, :] + totals[:, 2, :]
    denom = totals[:, 3, :] + totals[:, 4, :] + totals[:, 5, :]
    even = lax.broadcasted_iota(jnp.int32, peak.shape, 0) % 2 == 0
    low = jnp.max(jnp.where(even, peak, -jnp.inf), axis=0, keepdims=True)
    high = jnp.max(jnp.where(even, -jnp.inf, peak), axis=0, keepdims=True)
    share = denom * jnp.exp(peak - jnp.where(even, low, high))
    low = jnp.sum(jnp.where(even, share, 0.0), axis=0, keepdims=True)
    high = jnp.sum(jnp.where(even, 0.0, share), axis=0, keepdims=True)
    share = (share / jnp.where(even, low, high)).T
    for xl in range(2):
        mixed = jnp.zeros((64, HD), F32)
        for i in range(xl, count, 2):
            mixed = mixed + in_ref[i, 0:64, :].astype(F32) * share[0:64, i : i + 1]
        mixed = mixed.astype(BF16)
        for i in range(16):
            out_ref[2 * i + xl] = mixed


def combine(parts):
    return pl.pallas_call(
        combine_kernel,
        out_shape=jax.ShapeDtypeStruct((32, 64, HD), BF16),
        compiler_params=pltpu.CompilerParams(vmem_limit_bytes=VMEM_LIMIT),
    )(parts)


def output_kernel(side_ref, att_ref, own_ref, other_ref, y_ref, square_ref):
    side = side_ref[0]
    total = jnp.zeros((320, 64), F32)
    for i in range(16):
        attention = jnp.concatenate(
            [att_ref[2 * i + side], att_ref[2 * i + 1 - side]], axis=1
        )
        weights = jnp.concatenate([own_ref[i], other_ref[i]], axis=1)
        total = total + lax.dot_general(
            weights, attention, (((1,), (1,)), ((), ())), preferred_element_type=F32
        )
    y_ref[...] = total.T
    squares = jnp.sum(total * total, axis=0, keepdims=True)
    for i in range(16):
        square_ref[i] = squares


def output_projection(side, attention, own, other):
    return pl.pallas_call(
        output_kernel,
        in_specs=[
            pl.BlockSpec(memory_space=pltpu.SMEM),
            *[pl.BlockSpec(memory_space=pltpu.VMEM)] * 3,
        ],
        out_shape=(
            jax.ShapeDtypeStruct((64, 320), F32),
            jax.ShapeDtypeStruct((16, 1, 64), F32),
        ),
        compiler_params=pltpu.CompilerParams(vmem_limit_bytes=VMEM_LIMIT),
    )(side, attention, own, other)


def to_owners(array, same):
    def device(g, xl, z):
        return ((g // 4 * 2 + xl) * 16 + z) * 4 + g % 4

    pairs = [
        (device(g, c // 16, c % 16), device(c // 2, c % 2 if same else 1 - c % 2, g))
        for g in range(16)
        for c in range(32)
    ]
    return lax.ppermute(array, ("y", "xl", "z", "xh", "core"), pairs)


def from_neighbour(array):
    return lax.ppermute(array, "z", [(z, z ^ 1) for z in range(16)])


def local(
    state,
    clean_tokens,
    w_query,
    w_key,
    w_value,
    w_out,
    cache_keys,
    cache_values,
    norm_gain,
    mod_gain,
    out_gain,
    levels,
    noise_index,
    placement,
    group_mask,
):
    flight, ch_dev, width = state.shape
    rows_count = flight * ch_dev

    side = lax.axis_index("xl")
    odd = lax.axis_index("z") % 2
    w_out_t = jnp.transpose(w_out)
    low, high = w_out_t[:, :HD], w_out_t[:, HD:]
    first = to_owners(jnp.where(odd == 0, low, high), True)
    second = to_owners(jnp.where(odd == 0, high, low), False)
    w_heads = jnp.concatenate([by_head(w) for w in (w_key, w_value, w_query)], axis=2)
    w_heads = swapped(w_heads, "xl").reshape(320, 3 * HD)
    w_columns = jnp.where(
        side == 0,
        jnp.concatenate([first, second], axis=0),
        jnp.concatenate([second, first], axis=0),
    )
    shard = jnp.concatenate([w_heads, w_columns], axis=1)
    w_full = lax.all_gather(shard, "z", axis=0, tiled=False)

    current = level_lookup(levels, noise_index)
    following = level_lookup(levels, noise_index + 1)
    rows = jnp.concatenate(
        [state.reshape(rows_count, width), clean_tokens.astype(F32)], axis=0
    )
    sigma_rows = jnp.concatenate(
        [jnp.repeat(current, ch_dev), jnp.zeros((ch_dev,), F32)]
    )
    squares = sent_to_all(jnp.sum(rows * rows, axis=1), WIDE).sum(axis=0)
    inverse = lax.rsqrt(squares / D + EPSILON)
    features = (
        rows
        * inverse[:, None]
        * norm_gain[None, :]
        * (1.0 + sigma_rows[:, None] * mod_gain[None, :])
    ).astype(BF16)
    features = sent_to_all(features, ("y", "xh", "xl"))
    features = sent_to_all(features, "core").reshape(2, 4, 2, 2, 80, width)

    table = jnp.arange(group_mask.shape[1], dtype=jnp.int32)
    held = (placement[:, None] == table[None, :]).astype(jnp.int32)
    seen = jnp.sum(held[None, :, :] * group_mask[:, None, :], axis=2) != 0
    seen = jnp.repeat(seen.T.astype(BF16), ch_dev, axis=1)
    seen = jnp.pad(jnp.concatenate([seen, seen], axis=1), ((0, 14), (0, 0)))
    kv = jnp.concatenate(
        [
            by_head(cache_keys),
            by_head(cache_values),
            jnp.broadcast_to(seen[None], (2, *seen.shape)),
        ],
        axis=1,
    )
    kv = swapped(kv, "xl")
    kv = (kv, from_neighbour(kv))
    values_t = [jnp.transpose(part[:, 512:1024], (0, 2, 1)) for part in kv]

    w_full, values_t = lax.optimization_barrier((w_full, values_t))
    queries = project(features, w_full, 2, HD, (16, 64, HD))
    queries = swapped(queries, "z").reshape(-1, HD)
    new = project(features, w_full, 0, 2 * HD, (320, HD))
    fresh = (new, from_neighbour(new))
    w_out_own = w_full[:, :, 3 * HD :]
    w_out_other = lax.ppermute(w_out_own, "xl", [(0, 1), (1, 0)])
    parts = attend(queries, kv, values_t, fresh)
    parts = swapped(parts, "z")
    attention = swapped(combine(parts), (*WIDE, "xl"))

    finished = new.reshape(2, 2, 80, HD)[:, :, 64:]
    mine = jnp.where(side == 0, finished[:, 0], finished[:, 1])
    other = jnp.where(side == 0, finished[:, 1], finished[:, 0])
    other = lax.ppermute(other, "xl", [(0, 1), (1, 0)])
    finished = jnp.where(
        side == 0,
        jnp.concatenate([mine, other], axis=2),
        jnp.concatenate([other, mine], axis=2),
    )
    new_keys, new_values = finished[0], finished[1]

    y, y_squares = output_projection(side.reshape(1), attention, w_out_own, w_out_other)
    y_squares = swapped(y_squares, WIDE).sum(axis=(0, 1))
    velocity = y * lax.rsqrt(y_squares / D + EPSILON)[:, None] * out_gain[None, :]
    new_state = state + (following - current)[:, None, None] * velocity.reshape(
        flight, ch_dev, width
    )
    return new_state, new_keys, new_values


def solution(mesh):
    fine = Mesh(mesh.devices.reshape(4, 2, 16, 2, 2), ("y", "xl", "z", "xh", "core"))
    in_specs = (
        P(None, CTX, WIDE),
        P(CTX, WIDE),
        P(CTX, WIDE),
        P(CTX, WIDE),
        P(CTX, WIDE),
        P(WIDE, CTX),
        P(CTX, WIDE),
        P(CTX, WIDE),
        P(WIDE),
        P(WIDE),
        P(WIDE),
        P(),
        P(),
        P(CTX),
        P(),
    )
    out_specs = (P(None, CTX, WIDE), P(CTX, WIDE), P(CTX, WIDE))
    return jax.shard_map(local, mesh=fine, in_specs=in_specs, out_specs=out_specs, check_vma=False)
```

```python
import functools
import math

import jax
import jax.numpy as jnp
from jax import lax
from jax.experimental import pallas as pl
from jax.experimental.pallas import tpu as pltpu
from jax.sharding import Mesh
from jax.sharding import PartitionSpec as P

D = 5120
HD = 128
SLOT = 256
EPSILON = 1e-06
VMEM_LIMIT = 56 * 1024 * 1024

CTX = ("xl", "z")
WIDE = ("y", "xh", "core")
BF16 = jnp.bfloat16
F32 = jnp.float32


def level_lookup(levels, indices):
    table = jnp.arange(levels.shape[0], dtype=jnp.int32)
    picked = (indices[:, None] == table[None, :]).astype(F32)
    return jnp.sum(picked * levels[None, :], axis=1)


def sent_to_all(array, axis):
    devices = lax.axis_size(axis)
    return lax.all_to_all(
        jnp.broadcast_to(array[None], (devices, *array.shape)), axis, 0, 0, tiled=True
    )


def swapped(blocks, axis):
    return lax.all_to_all(blocks, axis, 0, 0, tiled=True)


def by_head(matrix):
    return jnp.stack([matrix[:, :HD], matrix[:, HD:]])


def project_kernel(h_ref, w_ref, out_ref, acc):
    step = pl.program_id(0)

    @pl.when(step == 0)
    def _():
        acc[...] = jnp.zeros_like(acc)

    total = acc[...]
    width = acc.shape[1]
    for xh in range(2):
        for core in range(2):
            rows = h_ref[core, step, xh].reshape(160, 320)
            at = 2 * (2 * xh + core)
            weights = w_ref[at : at + 2].reshape(320, width)
            total = total + jnp.dot(rows, weights, preferred_element_type=F32)
    acc[...] = total

    @pl.when(step == pl.num_programs(0) - 1)
    def _():
        if width == HD:
            for xl in range(2):
                rows = total[80 * xl : 80 * xl + 64].astype(BF16)
                for i in range(8):
                    out_ref[2 * i + xl] = rows
        else:
            out_ref[0:160, :] = total[:, 0:HD].astype(BF16)
            out_ref[160:320, :] = total[:, HD:].astype(BF16)


def project(features, weights, block, width, shape):
    return pl.pallas_call(
        project_kernel,
        grid=(4,),
        in_specs=[
            pl.BlockSpec(memory_space=pltpu.VMEM),
            pl.BlockSpec((8, 160, width), lambda s: (s % 2, s // 2, block)),
        ],
        out_specs=pl.BlockSpec(shape, lambda s: (0,) * len(shape)),
        out_shape=jax.ShapeDtypeStruct(shape, BF16),
        scratch_shapes=[pltpu.VMEM((160, width), F32)],
        compiler_params=pltpu.CompilerParams(vmem_limit_bytes=VMEM_LIMIT),
        cost_estimate=pl.CostEstimate(
            flops=2 * 160 * D * width, bytes_accessed=4 * 2**20, transcendentals=0
        ),
    )(features, weights)


def in_three(value):
    high = value.astype(BF16).astype(F32)
    middle = (value - high).astype(BF16).astype(F32)
    return [high, middle, value - high - middle]


def pack_kernel(side_ref, keys_ref, values_ref, seen_ref, own_ref, other_ref):
    first = side_ref[0] == 0
    for ref, at in ((keys_ref, 0), (values_ref, 512)):
        low, high = ref[:, :HD], ref[:, HD:]
        own_ref[at : at + 512, :] = jnp.where(first, low, high)
        other_ref[at : at + 512, :] = jnp.where(first, high, low)
    own_ref[1024:1040, :] = seen_ref[...]
    other_ref[1024:1040, :] = seen_ref[...]


def pack(side, keys, values, seen):
    return pl.pallas_call(
        pack_kernel,
        in_specs=[
            pl.BlockSpec(memory_space=pltpu.SMEM),
            *[pl.BlockSpec(memory_space=pltpu.VMEM)] * 3,
        ],
        out_shape=(jax.ShapeDtypeStruct((1040, HD), BF16),) * 2,
        compiler_params=pltpu.CompilerParams(vmem_limit_bytes=VMEM_LIMIT),
        cost_estimate=pl.CostEstimate(flops=0, bytes_accessed=2**20, transcendentals=0),
    )(side, keys, values, seen)


def turn_kernel(own_ref, other_ref, out_ref):
    ones = (lax.broadcasted_iota(jnp.int32, (16, 512), 0) == 0).astype(F32).astype(BF16)
    for i, ref in enumerate((own_ref, other_ref)):
        for side in range(2):
            out_ref[i, side, 0:HD] = ref[side, 512:1024, :].astype(F32).T.astype(BF16)
            out_ref[i, side, HD : HD + 16] = ones


def turn(kv):
    return pl.pallas_call(
        turn_kernel,
        out_shape=jax.ShapeDtypeStruct((2, 2, HD + 16, 512), BF16),
        compiler_params=pltpu.CompilerParams(vmem_limit_bytes=VMEM_LIMIT),
        cost_estimate=pl.CostEstimate(flops=0, bytes_accessed=2**20, transcendentals=0),
    )(*kv)


def attend_kernel(q_ref, own_ref, other_ref, vt_ref, own_new, other_new, out_ref, fresh_vt):
    @pl.when(pl.program_id(0) == 0)
    def _():
        ones = (lax.broadcasted_iota(jnp.int32, (16, 160), 0) == 0).astype(F32)
        for i, new in enumerate((own_new, other_new)):
            fresh_vt[i, 0:HD] = new[160:320, :].astype(F32).T.astype(BF16)
            fresh_vt[i, HD : HD + 16] = ones.astype(BF16)

    scale = 1.0 / math.sqrt(HD)
    queries = q_ref[...]
    lanes = queries.shape[0]
    across = (((1,), (1,)), ((), ()))

    def products(keys):
        return lax.dot_general(keys, queries, across, preferred_element_type=F32)

    token = lax.broadcasted_iota(jnp.int32, (160, lanes), 0)
    lane = lax.broadcasted_iota(jnp.int32, (160, lanes), 1)
    token = jnp.where(token >= 80, token - 80, token)
    visible = (token >= 64) | ((token >> 4) <= ((lane & 63) >> 4))

    parts, values = [], []
    for i, (kv_ref, new) in enumerate(((own_ref, own_new), (other_ref, other_new))):
        for side in range(2):
            seen = kv_ref[side, 1024:1040, :].astype(F32)
            hidden = jnp.where(seen > 0.5, 0.0, -jnp.inf)
            hidden = jnp.concatenate([hidden] * (lanes // HD), axis=1)
            for slot in range(2):
                at = slice(slot * SLOT, (slot + 1) * SLOT)
                parts.append(products(kv_ref[side, at, :]) + hidden[slot : slot + 1, :])
                values.append(vt_ref[i, side, :, at])
        parts.append(jnp.where(visible, products(new[0:160, :]), -jnp.inf))
        values.append(fresh_vt[i])

    top = functools.reduce(
        jnp.maximum, [jnp.max(part, axis=0, keepdims=True) for part in parts]
    )
    factor = scale * math.log2(math.e)
    shift = top * factor
    total = jnp.zeros((HD + 16, lanes), F32)
    for part, value in zip(parts, values):
        weights = jnp.exp2(part * factor - shift).astype(BF16)
        total = total + jnp.dot(value, weights, preferred_element_type=F32)
    peak, denom = top * scale, total[HD : HD + 1]
    mean = (total[0:HD] / denom).T.astype(BF16)
    totals = jnp.concatenate(
        [*in_three(peak), *in_three(denom), jnp.zeros((10, lanes), F32)], axis=0
    )
    for block in range(lanes // 64):
        at = slice(block * 64, (block + 1) * 64)
        out_ref[block, 0:64, :] = mean[at, :]
        out_ref[block, 64:80, :] = jnp.concatenate(
            [totals[:, at], totals[:, at]], axis=1
        ).astype(BF16)


def attend(queries, kv, values_t, fresh):
    step = 256
    rows = queries.shape[0]
    arrays = (*kv, values_t, *fresh)

    def whole(array):
        return pl.BlockSpec(array.shape, lambda s: (0,) * array.ndim)

    return pl.pallas_call(
        attend_kernel,
        grid=(rows // step,),
        in_specs=[
            pl.BlockSpec((step, HD), lambda s: (s, 0)),
            *[whole(array) for array in arrays],
        ],
        out_specs=pl.BlockSpec((step // 64, 80, HD), lambda s: (s, 0, 0)),
        out_shape=jax.ShapeDtypeStruct((rows // 64, 80, HD), BF16),
        scratch_shapes=[pltpu.VMEM((2, HD + 16, 160), BF16)],
        compiler_params=pltpu.CompilerParams(vmem_limit_bytes=VMEM_LIMIT),
        cost_estimate=pl.CostEstimate(
            flops=4 * rows * 2368 * HD,
            bytes_accessed=3 * 2**20,
            transcendentals=rows * 2368,
        ),
    )(queries, *arrays)


def combine_kernel(in_ref, out_ref):
    count = in_ref.shape[0]
    totals = in_ref[:, 64:80, :].astype(F32)
    peak = totals[:, 0, :] + totals[:, 1, :] + totals[:, 2, :]
    denom = totals[:, 3, :] + totals[:, 4, :] + totals[:, 5, :]
    even = lax.broadcasted_iota(jnp.int32, peak.shape, 0) % 2 == 0
    low = jnp.max(jnp.where(even, peak, -jnp.inf), axis=0, keepdims=True)
    high = jnp.max(jnp.where(even, -jnp.inf, peak), axis=0, keepdims=True)
    share = denom * jnp.exp(peak - jnp.where(even, low, high))
    low = jnp.sum(jnp.where(even, share, 0.0), axis=0, keepdims=True)
    high = jnp.sum(jnp.where(even, 0.0, share), axis=0, keepdims=True)
    share = (share / jnp.where(even, low, high)).T
    for xl in range(2):
        mixed = jnp.zeros((64, HD), F32)
        for i in range(xl, count, 2):
            mixed = mixed + in_ref[i, 0:64, :].astype(F32) * share[0:64, i : i + 1]
        mixed = mixed.astype(BF16)
        for i in range(16):
            out_ref[2 * i + xl] = mixed


def combine(parts):
    return pl.pallas_call(
        combine_kernel,
        out_shape=jax.ShapeDtypeStruct((32, 64, HD), BF16),
        compiler_params=pltpu.CompilerParams(vmem_limit_bytes=VMEM_LIMIT),
    )(parts)


def output_kernel(att_ref, w_ref, y_ref, square_ref):
    total = jnp.zeros((320, 64), F32)
    for i in range(16):
        attention = jnp.concatenate([att_ref[2 * i], att_ref[2 * i + 1]], axis=1)
        total = total + lax.dot_general(
            w_ref[i], attention, (((1,), (1,)), ((), ())), preferred_element_type=F32
        )
    y_ref[...] = total.T
    squares = jnp.sum(total * total, axis=0, keepdims=True)
    for i in range(16):
        square_ref[i] = squares


def output_projection(attention, weights):
    return pl.pallas_call(
        output_kernel,
        out_shape=(
            jax.ShapeDtypeStruct((64, 320), F32),
            jax.ShapeDtypeStruct((16, 1, 64), F32),
        ),
        compiler_params=pltpu.CompilerParams(vmem_limit_bytes=VMEM_LIMIT),
    )(attention, weights)


def to_owners(array, same):
    def device(g, xl, z):
        return ((g // 4 * 2 + xl) * 16 + z) * 4 + g % 4

    pairs = [
        (device(g, c // 16, c % 16), device(c // 2, c % 2 if same else 1 - c % 2, g))
        for g in range(16)
        for c in range(32)
    ]
    return lax.ppermute(array, ("y", "xl", "z", "xh", "core"), pairs)


def from_neighbour(array):
    return lax.ppermute(array, "z", [(z, z ^ 1) for z in range(16)])


def local(
    state,
    clean_tokens,
    w_query,
    w_key,
    w_value,
    w_out,
    cache_keys,
    cache_values,
    norm_gain,
    mod_gain,
    out_gain,
    levels,
    noise_index,
    placement,
    group_mask,
):
    flight, ch_dev, width = state.shape
    rows_count = flight * ch_dev

    side = lax.axis_index("xl")
    w_heads = jnp.concatenate([by_head(w) for w in (w_key, w_value, w_query)], axis=2)
    w_heads, cache_keys, cache_values = lax.optimization_barrier(
        (swapped(w_heads, "xl"), cache_keys, cache_values)
    )
    w_heads = w_heads.reshape(320, 3 * HD)
    w_full = lax.all_gather(w_heads, "z", axis=0, tiled=False)

    current = level_lookup(levels, noise_index)
    following = level_lookup(levels, noise_index + 1)
    rows = jnp.concatenate(
        [state.reshape(rows_count, width), clean_tokens.astype(F32)], axis=0
    )
    sigma_rows = jnp.concatenate(
        [jnp.repeat(current, ch_dev), jnp.zeros((ch_dev,), F32)]
    )
    squares = sent_to_all(jnp.sum(rows * rows, axis=1), WIDE).sum(axis=0)
    inverse = lax.rsqrt(squares / D + EPSILON)
    features = (
        rows
        * inverse[:, None]
        * norm_gain[None, :]
        * (1.0 + sigma_rows[:, None] * mod_gain[None, :])
    ).astype(BF16)
    features, w_out = lax.optimization_barrier((features, w_out))
    w_out = jnp.transpose(w_out)
    first, second = to_owners(w_out, True), to_owners(w_out, False)
    features = sent_to_all(features, ("y", "xh", "xl"))
    features, first, second = lax.optimization_barrier((features, first, second))
    features = sent_to_all(features, "core").reshape(2, 4, 2, 2, 80, width)

    table = jnp.arange(group_mask.shape[1], dtype=jnp.int32)
    held = (placement[:, None] == table[None, :]).astype(jnp.int32)
    seen = jnp.sum(held[None, :, :] * group_mask[:, None, :], axis=2) != 0
    seen = jnp.repeat(seen.T.astype(BF16), ch_dev, axis=1)
    seen = jnp.pad(jnp.concatenate([seen, seen], axis=1), ((0, 14), (0, 0)))
    kv_own, kv_other = pack(side.reshape(1), cache_keys, cache_values, seen)
    kv_other = lax.ppermute(kv_other, "xl", [(0, 1), (1, 0)])
    kv = jnp.stack([kv_own, kv_other])
    kv = (kv, from_neighbour(kv))
    values_t = turn(kv)

    w_columns = jnp.where(
        side == 0,
        jnp.concatenate([first, second], axis=0),
        jnp.concatenate([second, first], axis=0),
    )
    w_out_full = lax.all_gather(w_columns, "z", axis=0, tiled=False)

    w_full, values_t = lax.optimization_barrier((w_full, values_t))
    queries = project(features, w_full, 2, HD, (16, 64, HD))
    queries = swapped(queries, "z").reshape(-1, HD)
    new = project(features, w_full, 0, 2 * HD, (320, HD))
    fresh = (new, from_neighbour(new))
    parts = attend(queries, kv, values_t, fresh)
    parts = swapped(parts, "z")
    attention = swapped(combine(parts), (*WIDE, "xl"))

    finished = new.reshape(2, 2, 80, HD)[:, :, 64:]
    mine = jnp.where(side == 0, finished[:, 0], finished[:, 1])
    other = jnp.where(side == 0, finished[:, 1], finished[:, 0])
    other = lax.ppermute(other, "xl", [(0, 1), (1, 0)])
    finished = jnp.where(
        side == 0,
        jnp.concatenate([mine, other], axis=2),
        jnp.concatenate([other, mine], axis=2),
    )
    new_keys, new_values = finished[0], finished[1]

    y, y_squares = output_projection(attention, w_out_full)
    y_squares = swapped(y_squares, WIDE).sum(axis=(0, 1))
    velocity = y * lax.rsqrt(y_squares / D + EPSILON)[:, None] * out_gain[None, :]
    new_state = state + (following - current)[:, None, None] * velocity.reshape(
        flight, ch_dev, width
    )
    return new_state, new_keys, new_values


def solution(mesh):
    fine = Mesh(mesh.devices.reshape(4, 2, 16, 2, 2), ("y", "xl", "z", "xh", "core"))
    in_specs = (
        P(None, CTX, WIDE),
        P(CTX, WIDE),
        P(CTX, WIDE),
        P(CTX, WIDE),
        P(CTX, WIDE),
        P(WIDE, CTX),
        P(CTX, WIDE),
        P(CTX, WIDE),
        P(WIDE),
        P(WIDE),
        P(WIDE),
        P(),
        P(),
        P(CTX),
        P(),
    )
    out_specs = (P(None, CTX, WIDE), P(CTX, WIDE), P(CTX, WIDE))
    return jax.shard_map(local, mesh=fine, in_specs=in_specs, out_specs=out_specs, check_vma=False)
```

```python
import functools
import math

import jax
import jax.numpy as jnp
from jax import lax
from jax.experimental import pallas as pl
from jax.experimental.pallas import tpu as pltpu
from jax.sharding import Mesh
from jax.sharding import PartitionSpec as P

D = 5120
HD = 128
SLOT = 256
EPSILON = 1e-06
VMEM_LIMIT = 56 * 1024 * 1024

CTX = ("xl", "z")
WIDE = ("y", "xh", "core")
BF16 = jnp.bfloat16
F32 = jnp.float32


def level_lookup(levels, indices):
    table = jnp.arange(levels.shape[0], dtype=jnp.int32)
    picked = (indices[:, None] == table[None, :]).astype(F32)
    return jnp.sum(picked * levels[None, :], axis=1)


def sent_to_all(array, axis):
    devices = lax.axis_size(axis)
    return lax.all_to_all(
        jnp.broadcast_to(array[None], (devices, *array.shape)), axis, 0, 0, tiled=True
    )


def swapped(blocks, axis):
    return lax.all_to_all(blocks, axis, 0, 0, tiled=True)


def by_head(matrix):
    return jnp.stack([matrix[:, :HD], matrix[:, HD:]])


def lay_out_kernel(h_ref, out_ref):
    for j in range(16):
        for xl in range(2):
            rows = h_ref[j % 2, j // 4, j // 2 % 2, xl]
            out_ref[80 * xl : 80 * (xl + 1), 320 * j : 320 * (j + 1)] = rows


def lay_out(features):
    return pl.pallas_call(
        lay_out_kernel,
        out_shape=jax.ShapeDtypeStruct((160, D), BF16),
        compiler_params=pltpu.CompilerParams(vmem_limit_bytes=VMEM_LIMIT),
        cost_estimate=pl.CostEstimate(flops=0, bytes_accessed=4 * 2**20, transcendentals=0),
    )(features)


def project_kernel(h_ref, w_ref, out_ref, acc):
    step = pl.program_id(0)
    width = acc.shape[1]
    weights = w_ref[...].reshape(D // 4, width)
    part = jnp.dot(h_ref[...], weights, preferred_element_type=F32)

    @pl.when(step == 0)
    def _():
        acc[...] = part

    @pl.when(step > 0)
    def _():
        acc[...] += part

    @pl.when(step == pl.num_programs(0) - 1)
    def _():
        total = acc[...]
        if width == HD:
            for xl in range(2):
                rows = total[80 * xl : 80 * xl + 64].astype(BF16)
                for i in range(8):
                    out_ref[2 * i + xl] = rows
        else:
            out_ref[0:160, :] = total[:, 0:HD].astype(BF16)
            out_ref[160:320, :] = total[:, HD:].astype(BF16)


def project(features, weights, block, width, shape):
    return pl.pallas_call(
        project_kernel,
        grid=(4,),
        in_specs=[
            pl.BlockSpec((160, D // 4), lambda s: (0, s)),
            pl.BlockSpec((8, 160, width), lambda s: (s % 2, s // 2, block)),
        ],
        out_specs=pl.BlockSpec(shape, lambda s: (0,) * len(shape)),
        out_shape=jax.ShapeDtypeStruct(shape, BF16),
        scratch_shapes=[pltpu.VMEM((160, width), F32)],
        compiler_params=pltpu.CompilerParams(vmem_limit_bytes=VMEM_LIMIT),
        cost_estimate=pl.CostEstimate(
            flops=2 * 160 * D * width, bytes_accessed=4 * 2**20, transcendentals=0
        ),
    )(features, weights)


def in_three(value):
    high = value.astype(BF16).astype(F32)
    middle = (value - high).astype(BF16).astype(F32)
    return [high, middle, value - high - middle]


def turn_kernel(own_ref, other_ref, out_ref):
    ones = (lax.broadcasted_iota(jnp.int32, (16, 512), 0) == 0).astype(F32).astype(BF16)
    for i, ref in enumerate((own_ref, other_ref)):
        for side in range(2):
            out_ref[i, side, 0:HD] = ref[side, 512:1024, :].astype(F32).T.astype(BF16)
            out_ref[i, side, HD : HD + 16] = ones


def turn(kv):
    return pl.pallas_call(
        turn_kernel,
        out_shape=jax.ShapeDtypeStruct((2, 2, HD + 16, 512), BF16),
        compiler_params=pltpu.CompilerParams(vmem_limit_bytes=VMEM_LIMIT),
        cost_estimate=pl.CostEstimate(flops=0, bytes_accessed=2**20, transcendentals=0),
    )(*kv)


def attend_kernel(q_ref, own_ref, other_ref, vt_ref, own_new, other_new, out_ref, fresh_vt):
    @pl.when(pl.program_id(0) == 0)
    def _():
        ones = (lax.broadcasted_iota(jnp.int32, (16, 160), 0) == 0).astype(F32)
        for i, new in enumerate((own_new, other_new)):
            fresh_vt[i, 0:HD] = new[160:320, :].astype(F32).T.astype(BF16)
            fresh_vt[i, HD : HD + 16] = ones.astype(BF16)

    scale = 1.0 / math.sqrt(HD)
    queries = q_ref[...]
    lanes = queries.shape[0]
    across = (((1,), (1,)), ((), ()))

    def products(keys):
        return lax.dot_general(keys, queries, across, preferred_element_type=F32)

    token = lax.broadcasted_iota(jnp.int32, (160, lanes), 0)
    lane = lax.broadcasted_iota(jnp.int32, (160, lanes), 1)
    token = jnp.where(token >= 80, token - 80, token)
    visible = (token >= 64) | ((token >> 4) <= ((lane & 63) >> 4))

    parts, values = [], []
    for i, (kv_ref, new) in enumerate(((own_ref, own_new), (other_ref, other_new))):
        for side in range(2):
            seen = kv_ref[side, 1024:1040, :].astype(F32)
            hidden = jnp.where(seen > 0.5, 0.0, -jnp.inf)
            hidden = jnp.concatenate([hidden] * (lanes // HD), axis=1)
            for slot in range(2):
                at = slice(slot * SLOT, (slot + 1) * SLOT)
                parts.append(products(kv_ref[side, at, :]) + hidden[slot : slot + 1, :])
                values.append(vt_ref[i, side, :, at])
        parts.append(jnp.where(visible, products(new[0:160, :]), -jnp.inf))
        values.append(fresh_vt[i])

    top = functools.reduce(
        jnp.maximum, [jnp.max(part, axis=0, keepdims=True) for part in parts]
    )
    factor = scale * math.log2(math.e)
    shift = top * factor
    total = jnp.zeros((HD + 16, lanes), F32)
    for part, value in zip(parts, values):
        weights = jnp.exp2(part * factor - shift).astype(BF16)
        total = total + jnp.dot(value, weights, preferred_element_type=F32)
    peak, denom = top * scale, total[HD : HD + 1]
    mean = (total[0:HD] / denom).T.astype(BF16)
    totals = jnp.concatenate(
        [*in_three(peak), *in_three(denom), jnp.zeros((10, lanes), F32)], axis=0
    )
    for block in range(lanes // 64):
        at = slice(block * 64, (block + 1) * 64)
        out_ref[block, 0:64, :] = mean[at, :]
        out_ref[block, 64:80, :] = jnp.concatenate(
            [totals[:, at], totals[:, at]], axis=1
        ).astype(BF16)


def attend(queries, kv, values_t, fresh):
    step = 256
    rows = queries.shape[0]
    arrays = (*kv, values_t, *fresh)

    def whole(array):
        return pl.BlockSpec(array.shape, lambda s: (0,) * array.ndim)

    return pl.pallas_call(
        attend_kernel,
        grid=(rows // step,),
        in_specs=[
            pl.BlockSpec((step, HD), lambda s: (s, 0)),
            *[whole(array) for array in arrays],
        ],
        out_specs=pl.BlockSpec((step // 64, 80, HD), lambda s: (s, 0, 0)),
        out_shape=jax.ShapeDtypeStruct((rows // 64, 80, HD), BF16),
        scratch_shapes=[pltpu.VMEM((2, HD + 16, 160), BF16)],
        compiler_params=pltpu.CompilerParams(vmem_limit_bytes=VMEM_LIMIT),
        cost_estimate=pl.CostEstimate(
            flops=4 * rows * 2368 * HD,
            bytes_accessed=3 * 2**20,
            transcendentals=rows * 2368,
        ),
    )(queries, *arrays)


def combine_kernel(in_ref, out_ref):
    count = in_ref.shape[0]
    totals = in_ref[:, 64:80, :].astype(F32)
    peak = totals[:, 0, :] + totals[:, 1, :] + totals[:, 2, :]
    denom = totals[:, 3, :] + totals[:, 4, :] + totals[:, 5, :]
    even = lax.broadcasted_iota(jnp.int32, peak.shape, 0) % 2 == 0
    low = jnp.max(jnp.where(even, peak, -jnp.inf), axis=0, keepdims=True)
    high = jnp.max(jnp.where(even, -jnp.inf, peak), axis=0, keepdims=True)
    share = denom * jnp.exp(peak - jnp.where(even, low, high))
    low = jnp.sum(jnp.where(even, share, 0.0), axis=0, keepdims=True)
    high = jnp.sum(jnp.where(even, 0.0, share), axis=0, keepdims=True)
    share = (share / jnp.where(even, low, high)).T
    for xl in range(2):
        mixed = jnp.zeros((64, HD), F32)
        for i in range(xl, count, 2):
            mixed = mixed + in_ref[i, 0:64, :].astype(F32) * share[0:64, i : i + 1]
        out_ref[64 * xl : 64 * (xl + 1)] = mixed.astype(BF16)


def combine(parts):
    return pl.pallas_call(
        combine_kernel,
        out_shape=jax.ShapeDtypeStruct((HD, HD), BF16),
        compiler_params=pltpu.CompilerParams(vmem_limit_bytes=VMEM_LIMIT),
    )(parts)


def output_kernel(att_ref, w_ref, out_ref):
    attention = att_ref[...]
    for m in range(8):
        weights = w_ref[2 * m : 2 * m + 2].reshape(320, HD)
        part = lax.dot_general(
            attention, weights, (((1,), (1,)), ((), ())), preferred_element_type=F32
        ).astype(BF16)
        out_ref[2 * m] = part[0:64]
        out_ref[2 * m + 1] = part[64:128]


def output_projection(attention, weights):
    return pl.pallas_call(
        output_kernel,
        grid=(2,),
        in_specs=[
            pl.BlockSpec((HD, HD), lambda s: (0, 0)),
            pl.BlockSpec((16, 160, HD), lambda s: (0, s, 3)),
        ],
        out_specs=pl.BlockSpec((16, 64, 320), lambda s: (s, 0, 0)),
        out_shape=jax.ShapeDtypeStruct((32, 64, 320), BF16),
        compiler_params=pltpu.CompilerParams(vmem_limit_bytes=VMEM_LIMIT),
    )(attention, weights)


def over_heads_kernel(in_ref, y_ref, square_ref):
    total = in_ref[0].astype(F32)
    for i in range(1, in_ref.shape[0]):
        total = total + in_ref[i].astype(F32)
    y_ref[...] = total
    squares = jnp.sum((total * total).T, axis=0, keepdims=True)
    for i in range(16):
        square_ref[i] = squares


def over_heads(parts):
    return pl.pallas_call(
        over_heads_kernel,
        out_shape=(
            jax.ShapeDtypeStruct((64, 320), F32),
            jax.ShapeDtypeStruct((16, 1, 64), F32),
        ),
        compiler_params=pltpu.CompilerParams(vmem_limit_bytes=VMEM_LIMIT),
    )(parts)


def from_neighbour(array):
    return lax.ppermute(array, "z", [(z, z ^ 1) for z in range(16)])


def local(
    state,
    clean_tokens,
    w_query,
    w_key,
    w_value,
    w_out,
    cache_keys,
    cache_values,
    norm_gain,
    mod_gain,
    out_gain,
    levels,
    noise_index,
    placement,
    group_mask,
):
    flight, ch_dev, width = state.shape
    rows_count = flight * ch_dev

    side = lax.axis_index("xl")
    parts = [by_head(w) for w in (w_key, w_value, w_query)]
    parts.append(jnp.transpose(w_out.reshape(2, HD, 160), (0, 2, 1)))
    shard = swapped(jnp.concatenate(parts, axis=2), "xl").reshape(320, 4 * HD)
    w_full = lax.all_gather(shard, "z", axis=0, tiled=False)

    current = level_lookup(levels, noise_index)
    following = level_lookup(levels, noise_index + 1)
    rows = jnp.concatenate(
        [state.reshape(rows_count, width), clean_tokens.astype(F32)], axis=0
    )
    sigma_rows = jnp.concatenate(
        [jnp.repeat(current, ch_dev), jnp.zeros((ch_dev,), F32)]
    )
    squares = sent_to_all(jnp.sum(rows * rows, axis=1), WIDE).sum(axis=0)
    inverse = lax.rsqrt(squares / D + EPSILON)
    features = (
        rows
        * inverse[:, None]
        * norm_gain[None, :]
        * (1.0 + sigma_rows[:, None] * mod_gain[None, :])
    ).astype(BF16)
    features = sent_to_all(features, ("y", "xh", "xl"))
    features = sent_to_all(features, "core").reshape(2, 4, 2, 2, 80, width)
    features = lay_out(features)

    table = jnp.arange(group_mask.shape[1], dtype=jnp.int32)
    held = (placement[:, None] == table[None, :]).astype(jnp.int32)
    seen = jnp.sum(held[None, :, :] * group_mask[:, None, :], axis=2) != 0
    seen = jnp.repeat(seen.T.astype(BF16), ch_dev, axis=1)
    seen = jnp.pad(jnp.concatenate([seen, seen], axis=1), ((0, 14), (0, 0)))
    kv = jnp.concatenate(
        [
            by_head(cache_keys),
            by_head(cache_values),
            jnp.broadcast_to(seen[None], (2, *seen.shape)),
        ],
        axis=1,
    )
    kv = swapped(kv, "xl")
    kv = (kv, from_neighbour(kv))
    values_t = turn(kv)

    w_full, values_t, features = lax.optimization_barrier((w_full, values_t, features))
    queries = project(features, w_full, 2, HD, (16, 64, HD))
    queries = swapped(queries, "z").reshape(-1, HD)
    new = project(features, w_full, 0, 2 * HD, (320, HD))
    fresh = (new, from_neighbour(new))
    parts = attend(queries, kv, values_t, fresh)
    parts = swapped(parts, "z")
    parts = swapped(output_projection(combine(parts), w_full), (*WIDE, "xl"))

    finished = new.reshape(2, 2, 80, HD)[:, :, 64:]
    mine = jnp.where(side == 0, finished[:, 0], finished[:, 1])
    other = jnp.where(side == 0, finished[:, 1], finished[:, 0])
    other = lax.ppermute(other, "xl", [(0, 1), (1, 0)])
    finished = jnp.where(
        side == 0,
        jnp.concatenate([mine, other], axis=2),
        jnp.concatenate([other, mine], axis=2),
    )
    new_keys, new_values = finished[0], finished[1]

    y, y_squares = over_heads(parts)
    y_squares = swapped(y_squares, WIDE).sum(axis=(0, 1))
    velocity = y * lax.rsqrt(y_squares / D + EPSILON)[:, None] * out_gain[None, :]
    new_state = state + (following - current)[:, None, None] * velocity.reshape(
        flight, ch_dev, width
    )
    return new_state, new_keys, new_values


def solution(mesh):
    fine = Mesh(mesh.devices.reshape(4, 2, 16, 2, 2), ("y", "xl", "z", "xh", "core"))
    in_specs = (
        P(None, CTX, WIDE),
        P(CTX, WIDE),
        P(CTX, WIDE),
        P(CTX, WIDE),
        P(CTX, WIDE),
        P(WIDE, CTX),
        P(CTX, WIDE),
        P(CTX, WIDE),
        P(WIDE),
        P(WIDE),
        P(WIDE),
        P(),
        P(),
        P(CTX),
        P(),
    )
    out_specs = (P(None, CTX, WIDE), P(CTX, WIDE), P(CTX, WIDE))
    return jax.shard_map(local, mesh=fine, in_specs=in_specs, out_specs=out_specs, check_vma=False)
```

```python
import functools
import math

import jax
import jax.numpy as jnp
from jax import lax
from jax.experimental import pallas as pl
from jax.experimental.pallas import tpu as pltpu
from jax.sharding import Mesh
from jax.sharding import PartitionSpec as P

D = 5120
HD = 128
SLOT = 256
EPSILON = 1e-06
VMEM_LIMIT = 56 * 1024 * 1024

CTX = ("xl", "z")
WIDE = ("y", "xh", "core")
BF16 = jnp.bfloat16
F32 = jnp.float32


def level_lookup(levels, indices):
    table = jnp.arange(levels.shape[0], dtype=jnp.int32)
    picked = (indices[:, None] == table[None, :]).astype(F32)
    return jnp.sum(picked * levels[None, :], axis=1)


def sent_to_all(array, axis):
    devices = lax.axis_size(axis)
    return lax.all_to_all(
        jnp.broadcast_to(array[None], (devices, *array.shape)), axis, 0, 0, tiled=True
    )


def swapped(blocks, axis):
    return lax.all_to_all(blocks, axis, 0, 0, tiled=True)


def by_head(matrix):
    return jnp.stack([matrix[:, :HD], matrix[:, HD:]])


def lay_out_kernel(h_ref, out_ref):
    for j in range(16):
        for xl in range(2):
            rows = h_ref[j % 2, j // 4, j // 2 % 2, xl]
            out_ref[80 * xl : 80 * (xl + 1), 320 * j : 320 * (j + 1)] = rows


def lay_out(features):
    return pl.pallas_call(
        lay_out_kernel,
        out_shape=jax.ShapeDtypeStruct((160, D), BF16),
        compiler_params=pltpu.CompilerParams(vmem_limit_bytes=VMEM_LIMIT),
        cost_estimate=pl.CostEstimate(flops=0, bytes_accessed=4 * 2**20, transcendentals=0),
    )(features)


def project_kernel(h_ref, w_ref, out_ref, acc):
    step = pl.program_id(0)
    width = acc.shape[1]
    weights = w_ref[...].reshape(D // 4, width)
    part = jnp.dot(h_ref[...], weights, preferred_element_type=F32)

    @pl.when(step == 0)
    def _():
        acc[...] = part

    @pl.when(step > 0)
    def _():
        acc[...] += part

    @pl.when(step == pl.num_programs(0) - 1)
    def _():
        total = acc[...]
        if width == HD:
            for xl in range(2):
                rows = total[80 * xl : 80 * xl + 64].astype(BF16)
                for i in range(8):
                    out_ref[2 * i + xl] = rows
        else:
            out_ref[0:160, :] = total[:, 0:HD].astype(BF16)
            out_ref[160:320, :] = total[:, HD:].astype(BF16)


def project(features, weights, block, width, shape):
    return pl.pallas_call(
        project_kernel,
        grid=(4,),
        in_specs=[
            pl.BlockSpec((160, D // 4), lambda s: (0, s)),
            pl.BlockSpec((8, 160, width), lambda s: (s % 2, s // 2, block)),
        ],
        out_specs=pl.BlockSpec(shape, lambda s: (0,) * len(shape)),
        out_shape=jax.ShapeDtypeStruct(shape, BF16),
        scratch_shapes=[pltpu.VMEM((160, width), F32)],
        compiler_params=pltpu.CompilerParams(vmem_limit_bytes=VMEM_LIMIT),
        cost_estimate=pl.CostEstimate(
            flops=2 * 160 * D * width, bytes_accessed=4 * 2**20, transcendentals=0
        ),
    )(features, weights)


def in_three(value):
    high = value.astype(BF16).astype(F32)
    middle = (value - high).astype(BF16).astype(F32)
    return [high, middle, value - high - middle]


def turn_kernel(kv_ref, out_ref):
    ones = (lax.broadcasted_iota(jnp.int32, (16, 512), 0) == 0).astype(F32).astype(BF16)
    for i in range(2):
        for side in range(2):
            values = kv_ref[side, i, 512:1024, :].astype(F32)
            out_ref[i, side, 0:HD] = values.T.astype(BF16)
            out_ref[i, side, HD : HD + 16] = ones


def turn(kv):
    return pl.pallas_call(
        turn_kernel,
        out_shape=jax.ShapeDtypeStruct((2, 2, HD + 16, 512), BF16),
        compiler_params=pltpu.CompilerParams(vmem_limit_bytes=VMEM_LIMIT),
        cost_estimate=pl.CostEstimate(flops=0, bytes_accessed=2**20, transcendentals=0),
    )(kv)


def attend_kernel(q_ref, kv_ref, vt_ref, own_new, other_new, out_ref, fresh_vt):
    @pl.when(pl.program_id(0) == 0)
    def _():
        ones = (lax.broadcasted_iota(jnp.int32, (16, 160), 0) == 0).astype(F32)
        for i, new in enumerate((own_new, other_new)):
            fresh_vt[i, 0:HD] = new[160:320, :].astype(F32).T.astype(BF16)
            fresh_vt[i, HD : HD + 16] = ones.astype(BF16)

    scale = 1.0 / math.sqrt(HD)
    queries = q_ref[...]
    lanes = queries.shape[0]
    across = (((1,), (1,)), ((), ()))

    def products(keys):
        return lax.dot_general(keys, queries, across, preferred_element_type=F32)

    token = lax.broadcasted_iota(jnp.int32, (160, lanes), 0)
    lane = lax.broadcasted_iota(jnp.int32, (160, lanes), 1)
    token = jnp.where(token >= 80, token - 80, token)
    visible = (token >= 64) | ((token >> 4) <= ((lane & 63) >> 4))

    parts, values = [], []
    for i, new in enumerate((own_new, other_new)):
        for side in range(2):
            seen = kv_ref[side, i, 1024:1040, :].astype(F32)
            hidden = jnp.where(seen > 0.5, 0.0, -jnp.inf)
            hidden = jnp.concatenate([hidden] * (lanes // HD), axis=1)
            for slot in range(2):
                at = slice(slot * SLOT, (slot + 1) * SLOT)
                parts.append(products(kv_ref[side, i, at, :]) + hidden[slot : slot + 1, :])
                values.append(vt_ref[i, side, :, at])
        parts.append(jnp.where(visible, products(new[0:160, :]), -jnp.inf))
        values.append(fresh_vt[i])

    top = functools.reduce(
        jnp.maximum, [jnp.max(part, axis=0, keepdims=True) for part in parts]
    )
    factor = scale * math.log2(math.e)
    shift = top * factor
    total = jnp.zeros((HD + 16, lanes), F32)
    for part, value in zip(parts, values):
        weights = jnp.exp2(part * factor - shift).astype(BF16)
        total = total + jnp.dot(value, weights, preferred_element_type=F32)
    peak, denom = top * scale, total[HD : HD + 1]
    mean = (total[0:HD] / denom).T.astype(BF16)
    totals = jnp.concatenate(
        [*in_three(peak), *in_three(denom), jnp.zeros((10, lanes), F32)], axis=0
    )
    for block in range(lanes // 64):
        at = slice(block * 64, (block + 1) * 64)
        out_ref[block, 0:64, :] = mean[at, :]
        out_ref[block, 64:80, :] = jnp.concatenate(
            [totals[:, at], totals[:, at]], axis=1
        ).astype(BF16)


def attend(queries, kv, values_t, fresh):
    step = 256
    rows = queries.shape[0]
    arrays = (kv, values_t, *fresh)

    def whole(array):
        return pl.BlockSpec(array.shape, lambda s: (0,) * array.ndim)

    return pl.pallas_call(
        attend_kernel,
        grid=(rows // step,),
        in_specs=[
            pl.BlockSpec((step, HD), lambda s: (s, 0)),
            *[whole(array) for array in arrays],
        ],
        out_specs=pl.BlockSpec((step // 64, 80, HD), lambda s: (s, 0, 0)),
        out_shape=jax.ShapeDtypeStruct((rows // 64, 80, HD), BF16),
        scratch_shapes=[pltpu.VMEM((2, HD + 16, 160), BF16)],
        compiler_params=pltpu.CompilerParams(vmem_limit_bytes=VMEM_LIMIT),
        cost_estimate=pl.CostEstimate(
            flops=4 * rows * 2368 * HD,
            bytes_accessed=3 * 2**20,
            transcendentals=rows * 2368,
        ),
    )(queries, *arrays)


def combine_kernel(in_ref, out_ref):
    count = in_ref.shape[0]
    totals = in_ref[:, 64:80, :].astype(F32)
    peak = totals[:, 0, :] + totals[:, 1, :] + totals[:, 2, :]
    denom = totals[:, 3, :] + totals[:, 4, :] + totals[:, 5, :]
    even = lax.broadcasted_iota(jnp.int32, peak.shape, 0) % 2 == 0
    low = jnp.max(jnp.where(even, peak, -jnp.inf), axis=0, keepdims=True)
    high = jnp.max(jnp.where(even, -jnp.inf, peak), axis=0, keepdims=True)
    share = denom * jnp.exp(peak - jnp.where(even, low, high))
    low = jnp.sum(jnp.where(even, share, 0.0), axis=0, keepdims=True)
    high = jnp.sum(jnp.where(even, 0.0, share), axis=0, keepdims=True)
    share = (share / jnp.where(even, low, high)).T
    for xl in range(2):
        mixed = jnp.zeros((64, HD), F32)
        for i in range(xl, count, 2):
            mixed = mixed + in_ref[i, 0:64, :].astype(F32) * share[0:64, i : i + 1]
        out_ref[64 * xl : 64 * (xl + 1)] = mixed.astype(BF16)


def combine(parts):
    return pl.pallas_call(
        combine_kernel,
        out_shape=jax.ShapeDtypeStruct((HD, HD), BF16),
        compiler_params=pltpu.CompilerParams(vmem_limit_bytes=VMEM_LIMIT),
    )(parts)


def output_kernel(att_ref, w_ref, out_ref):
    attention = att_ref[...]
    for m in range(8):
        weights = w_ref[2 * m : 2 * m + 2].reshape(320, HD)
        part = lax.dot_general(
            attention, weights, (((1,), (1,)), ((), ())), preferred_element_type=F32
        ).astype(BF16)
        for xl in range(2):
            block, at = part[64 * xl : 64 * (xl + 1)], 2 * m + xl
            out_ref[at, 0:64] = block[:, 0:HD]
            out_ref[at, 64:128] = block[:, HD : 2 * HD]
            out_ref[at, 128:160] = jnp.concatenate(
                [block[0:32, 2 * HD :], block[32:64, 2 * HD :]], axis=1
            )


def output_projection(attention, weights):
    return pl.pallas_call(
        output_kernel,
        grid=(2,),
        in_specs=[
            pl.BlockSpec((HD, HD), lambda s: (0, 0)),
            pl.BlockSpec((16, 160, HD), lambda s: (0, s, 0)),
        ],
        out_specs=pl.BlockSpec((16, 160, HD), lambda s: (s, 0, 0)),
        out_shape=jax.ShapeDtypeStruct((32, 160, HD), BF16),
        compiler_params=pltpu.CompilerParams(vmem_limit_bytes=VMEM_LIMIT),
    )(attention, weights)


def over_heads_kernel(in_ref, y_ref, square_ref):
    total = in_ref[0].astype(F32)
    for i in range(1, in_ref.shape[0]):
        total = total + in_ref[i].astype(F32)
    last = jnp.concatenate([total[128:160, 0:64], total[128:160, 64:128]], axis=0)
    y = jnp.concatenate([total[0:64], total[64:128], last], axis=1)
    y_ref[...] = y
    squares = jnp.sum((y * y).T, axis=0, keepdims=True)
    for i in range(16):
        square_ref[i] = squares


def over_heads(parts):
    return pl.pallas_call(
        over_heads_kernel,
        out_shape=(
            jax.ShapeDtypeStruct((64, 320), F32),
            jax.ShapeDtypeStruct((16, 1, 64), F32),
        ),
        compiler_params=pltpu.CompilerParams(vmem_limit_bytes=VMEM_LIMIT),
    )(parts)


def from_neighbour(array):
    return lax.ppermute(array, "z", [(z, z ^ 1) for z in range(16)])


def local(
    state,
    clean_tokens,
    w_query,
    w_key,
    w_value,
    w_out,
    cache_keys,
    cache_values,
    norm_gain,
    mod_gain,
    out_gain,
    levels,
    noise_index,
    placement,
    group_mask,
):
    flight, ch_dev, width = state.shape
    rows_count = flight * ch_dev

    near_keys, near_values = from_neighbour(cache_keys), from_neighbour(cache_values)

    side = lax.axis_index("xl")
    w_heads = jnp.concatenate([by_head(w) for w in (w_key, w_value, w_query)], axis=2)
    w_heads, w_out, near_keys, near_values = lax.optimization_barrier(
        (swapped(w_heads, "xl"), w_out, near_keys, near_values)
    )
    w_full = lax.all_gather(w_heads.reshape(320, 3 * HD), "z", axis=0, tiled=False)

    current = level_lookup(levels, noise_index)
    following = level_lookup(levels, noise_index + 1)
    rows = jnp.concatenate(
        [state.reshape(rows_count, width), clean_tokens.astype(F32)], axis=0
    )
    sigma_rows = jnp.concatenate(
        [jnp.repeat(current, ch_dev), jnp.zeros((ch_dev,), F32)]
    )
    squares = sent_to_all(jnp.sum(rows * rows, axis=1), WIDE).sum(axis=0)
    inverse = lax.rsqrt(squares / D + EPSILON)
    features = (
        rows
        * inverse[:, None]
        * norm_gain[None, :]
        * (1.0 + sigma_rows[:, None] * mod_gain[None, :])
    ).astype(BF16)
    features = sent_to_all(features, ("y", "xh", "xl"))
    features = sent_to_all(features, "core").reshape(2, 4, 2, 2, 80, width)
    features = lay_out(features)

    table = jnp.arange(group_mask.shape[1], dtype=jnp.int32)
    held = (placement[:, None] == table[None, :]).astype(jnp.int32)
    seen = jnp.sum(held[None, :, :] * group_mask[:, None, :], axis=2) != 0
    seen = jnp.repeat(seen.T.astype(BF16), ch_dev, axis=1)
    seen = jnp.pad(jnp.concatenate([seen, seen], axis=1), ((0, 14), (0, 0)))
    kv = jnp.concatenate(
        [
            by_head(cache_keys),
            by_head(cache_values),
            jnp.broadcast_to(seen[None], (2, *seen.shape)),
            by_head(near_keys),
            by_head(near_values),
            jnp.broadcast_to(from_neighbour(seen)[None], (2, *seen.shape)),
        ],
        axis=1,
    )
    kv = swapped(kv, "xl").reshape(2, 2, 1040, HD)
    values_t = turn(kv)

    low, high = jnp.transpose(w_out[:HD]), jnp.transpose(w_out[HD:])
    mine = jnp.where(side == 0, low, high)
    other = lax.ppermute(jnp.where(side == 0, high, low), "xl", [(0, 1), (1, 0)])
    w_columns = jnp.where(
        side == 0,
        jnp.concatenate([mine, other], axis=0),
        jnp.concatenate([other, mine], axis=0),
    )
    w_out_full = lax.all_gather(w_columns, "z", axis=0, tiled=False)

    w_full, values_t, features = lax.optimization_barrier((w_full, values_t, features))
    queries = project(features, w_full, 2, HD, (16, 64, HD))
    queries = swapped(queries, "z").reshape(-1, HD)
    new = project(features, w_full, 0, 2 * HD, (320, HD))
    fresh = (new, from_neighbour(new))
    parts = attend(queries, kv, values_t, fresh)
    parts = swapped(parts, "z")
    parts = swapped(output_projection(combine(parts), w_out_full), (*WIDE, "xl"))

    finished = new.reshape(2, 2, 80, HD)[:, :, 64:]
    mine = jnp.where(side == 0, finished[:, 0], finished[:, 1])
    other = jnp.where(side == 0, finished[:, 1], finished[:, 0])
    other = lax.ppermute(other, "xl", [(0, 1), (1, 0)])
    finished = jnp.where(
        side == 0,
        jnp.concatenate([mine, other], axis=2),
        jnp.concatenate([other, mine], axis=2),
    )
    new_keys, new_values = finished[0], finished[1]

    y, y_squares = over_heads(parts)
    y_squares = swapped(y_squares, WIDE).sum(axis=(0, 1))
    velocity = y * lax.rsqrt(y_squares / D + EPSILON)[:, None] * out_gain[None, :]
    new_state = state + (following - current)[:, None, None] * velocity.reshape(
        flight, ch_dev, width
    )
    return new_state, new_keys, new_values


def solution(mesh):
    fine = Mesh(mesh.devices.reshape(4, 2, 16, 2, 2), ("y", "xl", "z", "xh", "core"))
    in_specs = (
        P(None, CTX, WIDE),
        P(CTX, WIDE),
        P(CTX, WIDE),
        P(CTX, WIDE),
        P(CTX, WIDE),
        P(WIDE, CTX),
        P(CTX, WIDE),
        P(CTX, WIDE),
        P(WIDE),
        P(WIDE),
        P(WIDE),
        P(),
        P(),
        P(CTX),
        P(),
    )
    out_specs = (P(None, CTX, WIDE), P(CTX, WIDE), P(CTX, WIDE))
    return jax.shard_map(local, mesh=fine, in_specs=in_specs, out_specs=out_specs, check_vma=False)
```

```python
import functools
import math

import jax
import jax.numpy as jnp
from jax import lax
from jax.experimental import pallas as pl
from jax.experimental.pallas import tpu as pltpu
from jax.sharding import Mesh
from jax.sharding import PartitionSpec as P

D = 5120
HD = 128
SLOT = 256
EPSILON = 1e-06
VMEM_LIMIT = 56 * 1024 * 1024

CTX = ("xl", "z")
WIDE = ("y", "xh", "core")
BF16 = jnp.bfloat16
F32 = jnp.float32


def level_lookup(levels, indices):
    table = jnp.arange(levels.shape[0], dtype=jnp.int32)
    picked = (indices[:, None] == table[None, :]).astype(F32)
    return jnp.sum(picked * levels[None, :], axis=1)


def sent_to_all(array, axis):
    devices = lax.axis_size(axis)
    return lax.all_to_all(
        jnp.broadcast_to(array[None], (devices, *array.shape)), axis, 0, 0, tiled=True
    )


def swapped(blocks, axis):
    return lax.all_to_all(blocks, axis, 0, 0, tiled=True)


def by_head(matrix):
    return jnp.stack([matrix[:, :HD], matrix[:, HD:]])


def lay_out_kernel(h_ref, out_ref):
    for j in range(16):
        for xl in range(2):
            rows = h_ref[j % 2, j // 4, j // 2 % 2, xl]
            out_ref[80 * xl : 80 * (xl + 1), 320 * j : 320 * (j + 1)] = rows


def lay_out(features):
    return pl.pallas_call(
        lay_out_kernel,
        out_shape=jax.ShapeDtypeStruct((160, D), BF16),
        compiler_params=pltpu.CompilerParams(vmem_limit_bytes=VMEM_LIMIT),
        cost_estimate=pl.CostEstimate(flops=0, bytes_accessed=4 * 2**20, transcendentals=0),
    )(features)


def project_kernel(h_ref, w_ref, out_ref, acc):
    step = pl.program_id(0)
    width = acc.shape[1]
    weights = w_ref[...].reshape(D // 4, width)
    part = jnp.dot(h_ref[...], weights, preferred_element_type=F32)

    @pl.when(step == 0)
    def _():
        acc[...] = part

    @pl.when(step > 0)
    def _():
        acc[...] += part

    @pl.when(step == pl.num_programs(0) - 1)
    def _():
        total = acc[...]
        if width == HD:
            for xl in range(2):
                rows = total[80 * xl : 80 * xl + 64].astype(BF16)
                for i in range(8):
                    out_ref[2 * i + xl] = rows
        else:
            out_ref[0:160, :] = total[:, 0:HD].astype(BF16)
            out_ref[160:320, :] = total[:, HD:].astype(BF16)


def project(features, weights, block, width, shape):
    return pl.pallas_call(
        project_kernel,
        grid=(4,),
        in_specs=[
            pl.BlockSpec((160, D // 4), lambda s: (0, s)),
            pl.BlockSpec((8, 160, width), lambda s: (s % 2, s // 2, block)),
        ],
        out_specs=pl.BlockSpec(shape, lambda s: (0,) * len(shape)),
        out_shape=jax.ShapeDtypeStruct(shape, BF16),
        scratch_shapes=[pltpu.VMEM((160, width), F32)],
        compiler_params=pltpu.CompilerParams(vmem_limit_bytes=VMEM_LIMIT),
        cost_estimate=pl.CostEstimate(
            flops=2 * 160 * D * width, bytes_accessed=4 * 2**20, transcendentals=0
        ),
    )(features, weights)


def in_three(value):
    high = value.astype(BF16).astype(F32)
    middle = (value - high).astype(BF16).astype(F32)
    return [high, middle, value - high - middle]


def turn_kernel(kv_ref, out_ref):
    ones = (lax.broadcasted_iota(jnp.int32, (16, 512), 0) == 0).astype(F32).astype(BF16)
    for i in range(2):
        for side in range(2):
            values = kv_ref[side, i, 512:1024, :].astype(F32)
            out_ref[i, side, 0:HD] = values.T.astype(BF16)
            out_ref[i, side, HD : HD + 16] = ones


def turn(kv):
    return pl.pallas_call(
        turn_kernel,
        out_shape=jax.ShapeDtypeStruct((2, 2, HD + 16, 512), BF16),
        compiler_params=pltpu.CompilerParams(vmem_limit_bytes=VMEM_LIMIT),
        cost_estimate=pl.CostEstimate(flops=0, bytes_accessed=2**20, transcendentals=0),
    )(kv)


def attend_kernel(q_ref, kv_ref, vt_ref, own_new, other_new, out_ref, fresh_vt):
    @pl.when(pl.program_id(0) == 0)
    def _():
        ones = (lax.broadcasted_iota(jnp.int32, (16, 160), 0) == 0).astype(F32)
        for i, new in enumerate((own_new, other_new)):
            fresh_vt[i, 0:HD] = new[160:320, :].astype(F32).T.astype(BF16)
            fresh_vt[i, HD : HD + 16] = ones.astype(BF16)

    scale = 1.0 / math.sqrt(HD)
    queries = q_ref[...]
    lanes = queries.shape[0]
    across = (((1,), (1,)), ((), ()))

    def products(keys):
        return lax.dot_general(keys, queries, across, preferred_element_type=F32)

    token = lax.broadcasted_iota(jnp.int32, (160, lanes), 0)
    lane = lax.broadcasted_iota(jnp.int32, (160, lanes), 1)
    token = jnp.where(token >= 80, token - 80, token)
    visible = (token >= 64) | ((token >> 4) <= ((lane & 63) >> 4))

    parts, values = [], []
    for i, new in enumerate((own_new, other_new)):
        for side in range(2):
            seen = kv_ref[side, i, 1024:1040, :].astype(F32)
            hidden = jnp.where(seen > 0.5, 0.0, -jnp.inf)
            hidden = jnp.concatenate([hidden] * (lanes // HD), axis=1)
            for slot in range(2):
                at = slice(slot * SLOT, (slot + 1) * SLOT)
                parts.append(products(kv_ref[side, i, at, :]) + hidden[slot : slot + 1, :])
                values.append(vt_ref[i, side, :, at])
        parts.append(jnp.where(visible, products(new[0:160, :]), -jnp.inf))
        values.append(fresh_vt[i])

    top = functools.reduce(
        jnp.maximum, [jnp.max(part, axis=0, keepdims=True) for part in parts]
    )
    factor = scale * math.log2(math.e)
    shift = top * factor
    total = jnp.zeros((HD + 16, lanes), F32)
    for part, value in zip(parts, values):
        weights = jnp.exp2(part * factor - shift).astype(BF16)
        total = total + jnp.dot(value, weights, preferred_element_type=F32)
    peak, denom = top * scale, total[HD : HD + 1]
    mean = (total[0:HD] / denom).T.astype(BF16)
    totals = jnp.concatenate(
        [*in_three(peak), *in_three(denom), jnp.zeros((10, lanes), F32)], axis=0
    )
    for block in range(lanes // 64):
        at = slice(block * 64, (block + 1) * 64)
        out_ref[block, 0:64, :] = mean[at, :]
        out_ref[block, 64:80, :] = jnp.concatenate(
            [totals[:, at], totals[:, at]], axis=1
        ).astype(BF16)


def attend(queries, kv, values_t, fresh):
    step = 256
    rows = queries.shape[0]
    arrays = (kv, values_t, *fresh)

    def whole(array):
        return pl.BlockSpec(array.shape, lambda s: (0,) * array.ndim)

    return pl.pallas_call(
        attend_kernel,
        grid=(rows // step,),
        in_specs=[
            pl.BlockSpec((step, HD), lambda s: (s, 0)),
            *[whole(array) for array in arrays],
        ],
        out_specs=pl.BlockSpec((step // 64, 80, HD), lambda s: (s, 0, 0)),
        out_shape=jax.ShapeDtypeStruct((rows // 64, 80, HD), BF16),
        scratch_shapes=[pltpu.VMEM((2, HD + 16, 160), BF16)],
        compiler_params=pltpu.CompilerParams(vmem_limit_bytes=VMEM_LIMIT),
        cost_estimate=pl.CostEstimate(
            flops=4 * rows * 2368 * HD,
            bytes_accessed=3 * 2**20,
            transcendentals=rows * 2368,
        ),
    )(queries, *arrays)


def combine(in_ref):
    totals = in_ref[:, 64:80, :].astype(F32)
    peak = totals[:, 0, :] + totals[:, 1, :] + totals[:, 2, :]
    denom = totals[:, 3, :] + totals[:, 4, :] + totals[:, 5, :]
    even = lax.broadcasted_iota(jnp.int32, peak.shape, 0) % 2 == 0
    low = jnp.max(jnp.where(even, peak, -jnp.inf), axis=0, keepdims=True)
    high = jnp.max(jnp.where(even, -jnp.inf, peak), axis=0, keepdims=True)
    share = denom * jnp.exp(peak - jnp.where(even, low, high))
    low = jnp.sum(jnp.where(even, share, 0.0), axis=0, keepdims=True)
    high = jnp.sum(jnp.where(even, 0.0, share), axis=0, keepdims=True)
    share = (share / jnp.where(even, low, high)).T
    for xl in range(2):
        mixed = jnp.zeros((64, HD), F32)
        for i in range(xl, in_ref.shape[0], 2):
            mixed = mixed + in_ref[i, 0:64, :].astype(F32) * share[0:64, i : i + 1]
        yield mixed.astype(BF16)


def output_kernel(in_ref, w_ref, out_ref, att):
    @pl.when(pl.program_id(0) == 0)
    def _():
        for xl, rows in enumerate(combine(in_ref)):
            att[64 * xl : 64 * (xl + 1)] = rows

    attention = att[...]
    for m in range(8):
        weights = w_ref[2 * m : 2 * m + 2].reshape(320, HD)
        part = lax.dot_general(
            attention, weights, (((1,), (1,)), ((), ())), preferred_element_type=F32
        ).astype(BF16)
        for xl in range(2):
            block, at = part[64 * xl : 64 * (xl + 1)], 2 * m + xl
            out_ref[at, 0:64] = block[:, 0:HD]
            out_ref[at, 64:128] = block[:, HD : 2 * HD]
            out_ref[at, 128:160] = jnp.concatenate(
                [block[0:32, 2 * HD :], block[32:64, 2 * HD :]], axis=1
            )


def output_projection(shares, weights):
    return pl.pallas_call(
        output_kernel,
        grid=(2,),
        in_specs=[
            pl.BlockSpec(shares.shape, lambda s: (0, 0, 0)),
            pl.BlockSpec((16, 160, HD), lambda s: (0, s, 3)),
        ],
        out_specs=pl.BlockSpec((16, 160, HD), lambda s: (s, 0, 0)),
        out_shape=jax.ShapeDtypeStruct((32, 160, HD), BF16),
        scratch_shapes=[pltpu.VMEM((HD, HD), BF16)],
        compiler_params=pltpu.CompilerParams(vmem_limit_bytes=VMEM_LIMIT),
    )(shares, weights)


def over_heads_kernel(in_ref, y_ref, square_ref):
    total = in_ref[0].astype(F32)
    for i in range(1, in_ref.shape[0]):
        total = total + in_ref[i].astype(F32)
    last = jnp.concatenate([total[128:160, 0:64], total[128:160, 64:128]], axis=0)
    y = jnp.concatenate([total[0:64], total[64:128], last], axis=1)
    y_ref[...] = y
    squares = jnp.sum((y * y).T, axis=0, keepdims=True)
    for i in range(16):
        square_ref[i] = squares


def over_heads(parts):
    return pl.pallas_call(
        over_heads_kernel,
        out_shape=(
            jax.ShapeDtypeStruct((64, 320), F32),
            jax.ShapeDtypeStruct((16, 1, 64), F32),
        ),
        compiler_params=pltpu.CompilerParams(vmem_limit_bytes=VMEM_LIMIT),
    )(parts)


def from_neighbour(array):
    return lax.ppermute(array, "z", [(z, z ^ 1) for z in range(16)])


def local(
    state,
    clean_tokens,
    w_query,
    w_key,
    w_value,
    w_out,
    cache_keys,
    cache_values,
    norm_gain,
    mod_gain,
    out_gain,
    levels,
    noise_index,
    placement,
    group_mask,
):
    flight, ch_dev, width = state.shape
    rows_count = flight * ch_dev

    tokens = jnp.concatenate([cache_keys, cache_values], axis=0)
    near = from_neighbour(tokens)

    side = lax.axis_index("xl")
    parts = [by_head(w) for w in (w_key, w_value, w_query)]
    parts.append(jnp.transpose(w_out.reshape(2, HD, 160), (0, 2, 1)))
    shard = swapped(jnp.concatenate(parts, axis=2), "xl")
    shard, near = lax.optimization_barrier((shard, near))
    w_full = lax.all_gather(shard.reshape(320, 4 * HD), "z", axis=0, tiled=False)

    current = level_lookup(levels, noise_index)
    following = level_lookup(levels, noise_index + 1)
    rows = jnp.concatenate(
        [state.reshape(rows_count, width), clean_tokens.astype(F32)], axis=0
    )
    sigma_rows = jnp.concatenate(
        [jnp.repeat(current, ch_dev), jnp.zeros((ch_dev,), F32)]
    )
    squares = sent_to_all(jnp.sum(rows * rows, axis=1), WIDE).sum(axis=0)
    inverse = lax.rsqrt(squares / D + EPSILON)
    features = (
        rows
        * inverse[:, None]
        * norm_gain[None, :]
        * (1.0 + sigma_rows[:, None] * mod_gain[None, :])
    ).astype(BF16)
    features = sent_to_all(features, ("y", "xh", "xl"))
    features = sent_to_all(features, "core").reshape(2, 4, 2, 2, 80, width)
    features = lay_out(features)

    table = jnp.arange(group_mask.shape[1], dtype=jnp.int32)
    held = (placement[:, None] == table[None, :]).astype(jnp.int32)
    seen = jnp.sum(held[None, :, :] * group_mask[:, None, :], axis=2) != 0
    seen = jnp.repeat(seen.T.astype(BF16), ch_dev, axis=1)
    seen = jnp.pad(jnp.concatenate([seen, seen], axis=1), ((0, 14), (0, 0)))
    kv = jnp.concatenate(
        [
            by_head(tokens),
            jnp.broadcast_to(seen[None], (2, *seen.shape)),
            by_head(near),
            jnp.broadcast_to(from_neighbour(seen)[None], (2, *seen.shape)),
        ],
        axis=1,
    )
    kv = swapped(kv, "xl").reshape(2, 2, 1040, HD)
    values_t = turn(kv)

    w_full, values_t, features = lax.optimization_barrier((w_full, values_t, features))
    queries = project(features, w_full, 2, HD, (16, 64, HD))
    queries = swapped(queries, "z").reshape(-1, HD)
    new = project(features, w_full, 0, 2 * HD, (320, HD))
    fresh = (new, from_neighbour(new))
    parts = attend(queries, kv, values_t, fresh)
    parts = swapped(parts, "z")
    parts = swapped(output_projection(parts, w_full), (*WIDE, "xl"))

    finished = new.reshape(2, 2, 80, HD)[:, :, 64:]
    mine = jnp.where(side == 0, finished[:, 0], finished[:, 1])
    other = jnp.where(side == 0, finished[:, 1], finished[:, 0])
    other = lax.ppermute(other, "xl", [(0, 1), (1, 0)])
    finished = jnp.where(
        side == 0,
        jnp.concatenate([mine, other], axis=2),
        jnp.concatenate([other, mine], axis=2),
    )
    new_keys, new_values = finished[0], finished[1]

    y, y_squares = over_heads(parts)
    y_squares = swapped(y_squares, WIDE).sum(axis=(0, 1))
    velocity = y * lax.rsqrt(y_squares / D + EPSILON)[:, None] * out_gain[None, :]
    new_state = state + (following - current)[:, None, None] * velocity.reshape(
        flight, ch_dev, width
    )
    return new_state, new_keys, new_values


def solution(mesh):
    fine = Mesh(mesh.devices.reshape(4, 2, 16, 2, 2), ("y", "xl", "z", "xh", "core"))
    in_specs = (
        P(None, CTX, WIDE),
        P(CTX, WIDE),
        P(CTX, WIDE),
        P(CTX, WIDE),
        P(CTX, WIDE),
        P(WIDE, CTX),
        P(CTX, WIDE),
        P(CTX, WIDE),
        P(WIDE),
        P(WIDE),
        P(WIDE),
        P(),
        P(),
        P(CTX),
        P(),
    )
    out_specs = (P(None, CTX, WIDE), P(CTX, WIDE), P(CTX, WIDE))
    return jax.shard_map(local, mesh=fine, in_specs=in_specs, out_specs=out_specs, check_vma=False)
```

```python
import functools
import math

import jax
import jax.numpy as jnp
from jax import lax
from jax.experimental import pallas as pl
from jax.experimental.pallas import tpu as pltpu
from jax.sharding import Mesh
from jax.sharding import PartitionSpec as P

D = 5120
HD = 128
SLOT = 256
EPSILON = 1e-06
VMEM_LIMIT = 56 * 1024 * 1024

CTX = ("xl", "z")
WIDE = ("y", "xh", "core")
BF16 = jnp.bfloat16
F32 = jnp.float32


def level_lookup(levels, indices):
    table = jnp.arange(levels.shape[0], dtype=jnp.int32)
    picked = (indices[:, None] == table[None, :]).astype(F32)
    return jnp.sum(picked * levels[None, :], axis=1)


def sent_to_all(array, axis):
    devices = lax.axis_size(axis)
    return lax.all_to_all(
        jnp.broadcast_to(array[None], (devices, *array.shape)), axis, 0, 0, tiled=True
    )


def swapped(blocks, axis):
    return lax.all_to_all(blocks, axis, 0, 0, tiled=True)


def by_head(matrix):
    return jnp.stack([matrix[:, :HD], matrix[:, HD:]])


def lay_out_kernel(h_ref, out_ref):
    for j in range(16):
        for xl in range(2):
            rows = h_ref[j % 2, j // 4, j // 2 % 2, xl]
            out_ref[80 * xl : 80 * (xl + 1), 320 * j : 320 * (j + 1)] = rows


def lay_out(features):
    return pl.pallas_call(
        lay_out_kernel,
        out_shape=jax.ShapeDtypeStruct((160, D), BF16),
        compiler_params=pltpu.CompilerParams(vmem_limit_bytes=VMEM_LIMIT),
        cost_estimate=pl.CostEstimate(flops=0, bytes_accessed=4 * 2**20, transcendentals=0),
    )(features)


def project_kernel(h_ref, w_ref, out_ref, acc):
    step = pl.program_id(0)
    width = acc.shape[1]
    weights = w_ref[...].reshape(D // 4, width)
    part = jnp.dot(h_ref[...], weights, preferred_element_type=F32)

    @pl.when(step == 0)
    def _():
        acc[...] = part

    @pl.when(step > 0)
    def _():
        acc[...] += part

    @pl.when(step == pl.num_programs(0) - 1)
    def _():
        total = acc[...]
        if width == HD:
            for xl in range(2):
                rows = total[80 * xl : 80 * xl + 64].astype(BF16)
                for i in range(8):
                    out_ref[2 * i + xl] = rows
        else:
            out_ref[0:160, :] = total[:, 0:HD].astype(BF16)
            out_ref[160:320, :] = total[:, HD:].astype(BF16)


def project(features, weights, block, width, shape):
    return pl.pallas_call(
        project_kernel,
        grid=(4,),
        in_specs=[
            pl.BlockSpec((160, D // 4), lambda s: (0, s)),
            pl.BlockSpec((8, 160, width), lambda s: (s % 2, s // 2, block)),
        ],
        out_specs=pl.BlockSpec(shape, lambda s: (0,) * len(shape)),
        out_shape=jax.ShapeDtypeStruct(shape, BF16),
        scratch_shapes=[pltpu.VMEM((160, width), F32)],
        compiler_params=pltpu.CompilerParams(vmem_limit_bytes=VMEM_LIMIT),
        cost_estimate=pl.CostEstimate(
            flops=2 * 160 * D * width, bytes_accessed=4 * 2**20, transcendentals=0
        ),
    )(features, weights)


def in_three(value):
    high = value.astype(BF16).astype(F32)
    middle = (value - high).astype(BF16).astype(F32)
    return [high, middle, value - high - middle]


def turn_kernel(kv_ref, out_ref):
    ones = (lax.broadcasted_iota(jnp.int32, (16, 512), 0) == 0).astype(F32).astype(BF16)
    for i in range(2):
        for side in range(2):
            values = kv_ref[side, i, 512:1024, :].astype(F32)
            out_ref[i, side, 0:HD] = values.T.astype(BF16)
            out_ref[i, side, HD : HD + 16] = ones


def turn(kv):
    return pl.pallas_call(
        turn_kernel,
        out_shape=jax.ShapeDtypeStruct((2, 2, HD + 16, 512), BF16),
        compiler_params=pltpu.CompilerParams(vmem_limit_bytes=VMEM_LIMIT),
        cost_estimate=pl.CostEstimate(flops=0, bytes_accessed=2**20, transcendentals=0),
    )(kv)


def attend_kernel(q_ref, kv_ref, vt_ref, own_new, other_new, out_ref, fresh_vt):
    @pl.when(pl.program_id(0) == 0)
    def _():
        ones = (lax.broadcasted_iota(jnp.int32, (16, 160), 0) == 0).astype(F32)
        for i, new in enumerate((own_new, other_new)):
            fresh_vt[i, 0:HD] = new[160:320, :].astype(F32).T.astype(BF16)
            fresh_vt[i, HD : HD + 16] = ones.astype(BF16)

    scale = 1.0 / math.sqrt(HD)
    queries = q_ref[...]
    lanes = queries.shape[0]
    across = (((1,), (1,)), ((), ()))

    def products(keys):
        return lax.dot_general(keys, queries, across, preferred_element_type=F32)

    token = lax.broadcasted_iota(jnp.int32, (160, lanes), 0)
    lane = lax.broadcasted_iota(jnp.int32, (160, lanes), 1)
    token = jnp.where(token >= 80, token - 80, token)
    visible = (token >= 64) | ((token >> 4) <= ((lane & 63) >> 4))

    parts, values = [], []
    for i, new in enumerate((own_new, other_new)):
        for side in range(2):
            seen = kv_ref[side, i, 1024:1040, :].astype(F32)
            hidden = jnp.where(seen > 0.5, 0.0, -jnp.inf)
            hidden = jnp.concatenate([hidden] * (lanes // HD), axis=1)
            for slot in range(2):
                at = slice(slot * SLOT, (slot + 1) * SLOT)
                parts.append(products(kv_ref[side, i, at, :]) + hidden[slot : slot + 1, :])
                values.append(vt_ref[i, side, :, at])
        parts.append(jnp.where(visible, products(new[0:160, :]), -jnp.inf))
        values.append(fresh_vt[i])

    top = functools.reduce(
        jnp.maximum, [jnp.max(part, axis=0, keepdims=True) for part in parts]
    )
    factor = scale * math.log2(math.e)
    shift = top * factor
    total = jnp.zeros((HD + 16, lanes), F32)
    for part, value in zip(parts, values):
        weights = jnp.exp2(part * factor - shift).astype(BF16)
        total = total + jnp.dot(value, weights, preferred_element_type=F32)
    peak, denom = top * scale, total[HD : HD + 1]
    mean = (total[0:HD] / denom).T.astype(BF16)
    totals = jnp.concatenate(
        [*in_three(peak), *in_three(denom), jnp.zeros((10, lanes), F32)], axis=0
    )
    for block in range(lanes // 64):
        at = slice(block * 64, (block + 1) * 64)
        out_ref[block, 0:64, :] = mean[at, :]
        out_ref[block, 64:80, :] = jnp.concatenate(
            [totals[:, at], totals[:, at]], axis=1
        ).astype(BF16)


def attend(queries, kv, values_t, fresh):
    step = 256
    rows = queries.shape[0]
    arrays = (kv, values_t, *fresh)

    def whole(array):
        return pl.BlockSpec(array.shape, lambda s: (0,) * array.ndim)

    return pl.pallas_call(
        attend_kernel,
        grid=(rows // step,),
        in_specs=[
            pl.BlockSpec((step, HD), lambda s: (s, 0)),
            *[whole(array) for array in arrays],
        ],
        out_specs=pl.BlockSpec((step // 64, 80, HD), lambda s: (s, 0, 0)),
        out_shape=jax.ShapeDtypeStruct((rows // 64, 80, HD), BF16),
        scratch_shapes=[pltpu.VMEM((2, HD + 16, 160), BF16)],
        compiler_params=pltpu.CompilerParams(vmem_limit_bytes=VMEM_LIMIT),
        cost_estimate=pl.CostEstimate(
            flops=4 * rows * 2368 * HD,
            bytes_accessed=3 * 2**20,
            transcendentals=rows * 2368,
        ),
    )(queries, *arrays)


def combine(in_ref):
    totals = in_ref[:, 64:80, :].astype(F32)
    peak = totals[:, 0, :] + totals[:, 1, :] + totals[:, 2, :]
    denom = totals[:, 3, :] + totals[:, 4, :] + totals[:, 5, :]
    even = lax.broadcasted_iota(jnp.int32, peak.shape, 0) % 2 == 0
    low = jnp.max(jnp.where(even, peak, -jnp.inf), axis=0, keepdims=True)
    high = jnp.max(jnp.where(even, -jnp.inf, peak), axis=0, keepdims=True)
    share = denom * jnp.exp(peak - jnp.where(even, low, high))
    low = jnp.sum(jnp.where(even, share, 0.0), axis=0, keepdims=True)
    high = jnp.sum(jnp.where(even, 0.0, share), axis=0, keepdims=True)
    share = (share / jnp.where(even, low, high)).T
    for xl in range(2):
        mixed = jnp.zeros((64, HD), F32)
        for i in range(xl, in_ref.shape[0], 2):
            mixed = mixed + in_ref[i, 0:64, :].astype(F32) * share[0:64, i : i + 1]
        yield mixed.astype(BF16)


def output_kernel(in_ref, w_ref, out_ref, att):
    @pl.when(pl.program_id(0) == 0)
    def _():
        for xl, rows in enumerate(combine(in_ref)):
            att[64 * xl : 64 * (xl + 1)] = rows

    attention = att[...]
    for m in range(8):
        weights = w_ref[2 * m : 2 * m + 2].reshape(320, HD)
        part = lax.dot_general(
            attention, weights, (((1,), (1,)), ((), ())), preferred_element_type=F32
        ).astype(BF16)
        for xl in range(2):
            block, at = part[64 * xl : 64 * (xl + 1)], 2 * (m // 2) + xl
            out_ref[m % 2, at, 0:64] = block[:, 0:HD]
            out_ref[m % 2, at, 64:128] = block[:, HD : 2 * HD]
            out_ref[m % 2, at, 128:160] = jnp.concatenate(
                [block[0:32, 2 * HD :], block[32:64, 2 * HD :]], axis=1
            )


def output_projection(shares, weights):
    return pl.pallas_call(
        output_kernel,
        grid=(2,),
        in_specs=[
            pl.BlockSpec(shares.shape, lambda s: (0, 0, 0)),
            pl.BlockSpec((16, 160, HD), lambda s: (0, s, 3)),
        ],
        out_specs=pl.BlockSpec((2, 8, 160, HD), lambda s: (0, s, 0, 0)),
        out_shape=jax.ShapeDtypeStruct((2, 16, 160, HD), BF16),
        scratch_shapes=[pltpu.VMEM((HD, HD), BF16)],
        compiler_params=pltpu.CompilerParams(vmem_limit_bytes=VMEM_LIMIT),
    )(shares, weights)


def over_heads_kernel(in_ref, y_ref, square_ref):
    total = in_ref[0].astype(F32)
    for i in range(1, in_ref.shape[0]):
        total = total + in_ref[i].astype(F32)
    last = jnp.concatenate([total[128:160, 0:64], total[128:160, 64:128]], axis=0)
    y = jnp.concatenate([total[0:64], total[64:128], last], axis=1)
    y_ref[...] = y
    squares = jnp.sum((y * y).T, axis=0, keepdims=True)
    for i in range(16):
        square_ref[i] = squares


def over_heads(parts):
    return pl.pallas_call(
        over_heads_kernel,
        out_shape=(
            jax.ShapeDtypeStruct((64, 320), F32),
            jax.ShapeDtypeStruct((16, 1, 64), F32),
        ),
        compiler_params=pltpu.CompilerParams(vmem_limit_bytes=VMEM_LIMIT),
    )(parts)


def from_neighbour(array):
    return lax.ppermute(array, "z", [(z, z ^ 1) for z in range(16)])


def local(
    state,
    clean_tokens,
    w_query,
    w_key,
    w_value,
    w_out,
    cache_keys,
    cache_values,
    norm_gain,
    mod_gain,
    out_gain,
    levels,
    noise_index,
    placement,
    group_mask,
):
    flight, ch_dev, width = state.shape
    rows_count = flight * ch_dev

    tokens = jnp.concatenate([cache_keys, cache_values], axis=0)
    near = from_neighbour(tokens)

    side = lax.axis_index("xl")
    parts = [by_head(w) for w in (w_key, w_value, w_query)]
    parts.append(jnp.transpose(w_out.reshape(2, HD, 160), (0, 2, 1)))
    shard = swapped(jnp.concatenate(parts, axis=2), "xl")
    shard, near = lax.optimization_barrier((shard, near))
    w_full = lax.all_gather(shard.reshape(320, 4 * HD), "z", axis=0, tiled=False)

    current = level_lookup(levels, noise_index)
    following = level_lookup(levels, noise_index + 1)
    rows = jnp.concatenate(
        [state.reshape(rows_count, width), clean_tokens.astype(F32)], axis=0
    )
    sigma_rows = jnp.concatenate(
        [jnp.repeat(current, ch_dev), jnp.zeros((ch_dev,), F32)]
    )
    squares = sent_to_all(jnp.sum(rows * rows, axis=1), WIDE).sum(axis=0)
    inverse = lax.rsqrt(squares / D + EPSILON)
    features = (
        rows
        * inverse[:, None]
        * norm_gain[None, :]
        * (1.0 + sigma_rows[:, None] * mod_gain[None, :])
    ).astype(BF16)
    features = sent_to_all(features, ("y", "xh", "xl"))
    features = sent_to_all(features, "core").reshape(2, 4, 2, 2, 80, width)
    features = lay_out(features)

    table = jnp.arange(group_mask.shape[1], dtype=jnp.int32)
    held = (placement[:, None] == table[None, :]).astype(jnp.int32)
    seen = jnp.sum(held[None, :, :] * group_mask[:, None, :], axis=2) != 0
    seen = jnp.repeat(seen.T.astype(BF16), ch_dev, axis=1)
    seen = jnp.pad(jnp.concatenate([seen, seen], axis=1), ((0, 14), (0, 0)))
    kv = jnp.concatenate(
        [
            by_head(tokens),
            jnp.broadcast_to(seen[None], (2, *seen.shape)),
            by_head(near),
            jnp.broadcast_to(from_neighbour(seen)[None], (2, *seen.shape)),
        ],
        axis=1,
    )
    kv = swapped(kv, "xl").reshape(2, 2, 1040, HD)
    values_t = turn(kv)

    w_full, values_t, features = lax.optimization_barrier((w_full, values_t, features))
    queries = project(features, w_full, 2, HD, (16, 64, HD))
    queries = swapped(queries, "z").reshape(-1, HD)
    new = project(features, w_full, 0, 2 * HD, (320, HD))
    fresh = (new, from_neighbour(new))
    parts = attend(queries, kv, values_t, fresh)
    parts = swapped(parts, "z")
    parts = swapped(output_projection(parts, w_full), "core")
    parts = swapped(parts[0] + parts[1], ("y", "xh", "xl"))

    finished = new.reshape(2, 2, 80, HD)[:, :, 64:]
    mine = jnp.where(side == 0, finished[:, 0], finished[:, 1])
    other = jnp.where(side == 0, finished[:, 1], finished[:, 0])
    other = lax.ppermute(other, "xl", [(0, 1), (1, 0)])
    finished = jnp.where(
        side == 0,
        jnp.concatenate([mine, other], axis=2),
        jnp.concatenate([other, mine], axis=2),
    )
    new_keys, new_values = finished[0], finished[1]

    y, y_squares = over_heads(parts)
    y_squares = swapped(y_squares, WIDE).sum(axis=(0, 1))
    velocity = y * lax.rsqrt(y_squares / D + EPSILON)[:, None] * out_gain[None, :]
    step = jnp.repeat(following - current, ch_dev)[:, None]
    new_state = state.reshape(rows_count, width) + step * velocity
    new_state = new_state.reshape(flight, ch_dev, width)
    return new_state, new_keys, new_values


def solution(mesh):
    fine = Mesh(mesh.devices.reshape(4, 2, 16, 2, 2), ("y", "xl", "z", "xh", "core"))
    in_specs = (
        P(None, CTX, WIDE),
        P(CTX, WIDE),
        P(CTX, WIDE),
        P(CTX, WIDE),
        P(CTX, WIDE),
        P(WIDE, CTX),
        P(CTX, WIDE),
        P(CTX, WIDE),
        P(WIDE),
        P(WIDE),
        P(WIDE),
        P(),
        P(),
        P(CTX),
        P(),
    )
    out_specs = (P(None, CTX, WIDE), P(CTX, WIDE), P(CTX, WIDE))
    return jax.shard_map(local, mesh=fine, in_specs=in_specs, out_specs=out_specs, check_vma=False)
```

```python
import functools
import math

import jax
import jax.numpy as jnp
from jax import lax
from jax.experimental import pallas as pl
from jax.experimental.pallas import tpu as pltpu
from jax.sharding import Mesh
from jax.sharding import PartitionSpec as P

D = 5120
HD = 128
SLOT = 256
EPSILON = 1e-06
VMEM_LIMIT = 56 * 1024 * 1024

CTX = ("xl", "z")
WIDE = ("y", "xh", "core")
BF16 = jnp.bfloat16
F32 = jnp.float32


def level_lookup(levels, indices):
    table = jnp.arange(levels.shape[0], dtype=jnp.int32)
    picked = (indices[:, None] == table[None, :]).astype(F32)
    return jnp.sum(picked * levels[None, :], axis=1)


def sent_to_all(array, axis):
    devices = lax.axis_size(axis)
    return lax.all_to_all(
        jnp.broadcast_to(array[None], (devices, *array.shape)), axis, 0, 0, tiled=True
    )


def swapped(blocks, axis):
    return lax.all_to_all(blocks, axis, 0, 0, tiled=True)


def by_head(matrix):
    return jnp.stack([matrix[:, :HD], matrix[:, HD:]])


def prepare_kernel(keys_ref, values_ref, k_ref, v_ref, q_ref, out_ref, tokens_ref, shard_ref):
    tokens_ref[0:512, :] = keys_ref[...]
    tokens_ref[512:1024, :] = values_ref[...]
    for head in range(2):
        at = slice(HD * head, HD * (head + 1))
        for i, ref in enumerate((k_ref, v_ref, q_ref, out_ref)):
            shard_ref[head, :, HD * i : HD * (i + 1)] = ref[:, at]


def prepare(*arrays):
    return pl.pallas_call(
        prepare_kernel,
        out_shape=(
            jax.ShapeDtypeStruct((1024, 2 * HD), BF16),
            jax.ShapeDtypeStruct((2, 160, 4 * HD), BF16),
        ),
        compiler_params=pltpu.CompilerParams(vmem_limit_bytes=VMEM_LIMIT),
        cost_estimate=pl.CostEstimate(flops=0, bytes_accessed=2 * 2**20, transcendentals=0),
    )(*arrays)


def lay_out_kernel(h_ref, out_ref):
    for j in range(16):
        for xl in range(2):
            rows = h_ref[j % 2, j // 4, j // 2 % 2, xl]
            out_ref[80 * xl : 80 * (xl + 1), 320 * j : 320 * (j + 1)] = rows


def lay_out(features):
    return pl.pallas_call(
        lay_out_kernel,
        out_shape=jax.ShapeDtypeStruct((160, D), BF16),
        compiler_params=pltpu.CompilerParams(vmem_limit_bytes=VMEM_LIMIT),
        cost_estimate=pl.CostEstimate(flops=0, bytes_accessed=4 * 2**20, transcendentals=0),
    )(features)


def project_kernel(h_ref, w_ref, out_ref, acc):
    step = pl.program_id(0)
    width = acc.shape[1]
    weights = w_ref[...].reshape(D // 2, width)
    part = jnp.dot(h_ref[...], weights, preferred_element_type=F32)

    @pl.when(step == 0)
    def _():
        acc[...] = part

    @pl.when(step > 0)
    def _():
        acc[...] += part

    @pl.when(step == pl.num_programs(0) - 1)
    def _():
        total = acc[...]
        if width == HD:
            for xl in range(2):
                rows = total[80 * xl : 80 * xl + 64].astype(BF16)
                for i in range(8):
                    out_ref[2 * i + xl] = rows
        else:
            out_ref[0:160, :] = total[:, 0:HD].astype(BF16)
            out_ref[160:320, :] = total[:, HD:].astype(BF16)


def project(features, weights, block, width, shape):
    return pl.pallas_call(
        project_kernel,
        grid=(2,),
        in_specs=[
            pl.BlockSpec((160, D // 2), lambda s: (0, s)),
            pl.BlockSpec((16, 160, width), lambda s: (0, s, block)),
        ],
        out_specs=pl.BlockSpec(shape, lambda s: (0,) * len(shape)),
        out_shape=jax.ShapeDtypeStruct(shape, BF16),
        scratch_shapes=[pltpu.VMEM((160, width), F32)],
        compiler_params=pltpu.CompilerParams(vmem_limit_bytes=VMEM_LIMIT),
        cost_estimate=pl.CostEstimate(
            flops=2 * 160 * D * width, bytes_accessed=4 * 2**20, transcendentals=0
        ),
    )(features, weights)


def in_three(value):
    high = value.astype(BF16).astype(F32)
    middle = (value - high).astype(BF16).astype(F32)
    return [high, middle, value - high - middle]


def turn_kernel(kv_ref, out_ref):
    ones = (lax.broadcasted_iota(jnp.int32, (16, 512), 0) == 0).astype(F32).astype(BF16)
    for i in range(2):
        for side in range(2):
            values = kv_ref[side, i, 512:1024, :].astype(F32)
            out_ref[i, side, 0:HD] = values.T.astype(BF16)
            out_ref[i, side, HD : HD + 16] = ones


def turn(kv):
    return pl.pallas_call(
        turn_kernel,
        out_shape=jax.ShapeDtypeStruct((2, 2, HD + 16, 512), BF16),
        compiler_params=pltpu.CompilerParams(vmem_limit_bytes=VMEM_LIMIT),
        cost_estimate=pl.CostEstimate(flops=0, bytes_accessed=2**20, transcendentals=0),
    )(kv)


def attend_kernel(q_ref, kv_ref, vt_ref, own_new, other_new, out_ref, fresh_vt):
    @pl.when(pl.program_id(0) == 0)
    def _():
        ones = (lax.broadcasted_iota(jnp.int32, (16, 160), 0) == 0).astype(F32)
        for i, new in enumerate((own_new, other_new)):
            fresh_vt[i, 0:HD] = new[160:320, :].astype(F32).T.astype(BF16)
            fresh_vt[i, HD : HD + 16] = ones.astype(BF16)

    scale = 1.0 / math.sqrt(HD)
    queries = q_ref[...]
    lanes = queries.shape[0]
    across = (((1,), (1,)), ((), ()))

    def products(keys):
        return lax.dot_general(keys, queries, across, preferred_element_type=F32)

    token = lax.broadcasted_iota(jnp.int32, (160, lanes), 0)
    lane = lax.broadcasted_iota(jnp.int32, (160, lanes), 1)
    token = jnp.where(token >= 80, token - 80, token)
    visible = (token >= 64) | ((token >> 4) <= ((lane & 63) >> 4))

    parts, values = [], []
    for i, new in enumerate((own_new, other_new)):
        for side in range(2):
            seen = kv_ref[side, i, 1024:1040, :].astype(F32)
            hidden = jnp.where(seen > 0.5, 0.0, -jnp.inf)
            hidden = jnp.concatenate([hidden] * (lanes // HD), axis=1)
            for slot in range(2):
                at = slice(slot * SLOT, (slot + 1) * SLOT)
                parts.append(products(kv_ref[side, i, at, :]) + hidden[slot : slot + 1, :])
                values.append(vt_ref[i, side, :, at])
        parts.append(jnp.where(visible, products(new[0:160, :]), -jnp.inf))
        values.append(fresh_vt[i])

    top = functools.reduce(
        jnp.maximum, [jnp.max(part, axis=0, keepdims=True) for part in parts]
    )
    factor = scale * math.log2(math.e)
    shift = top * factor
    total = jnp.zeros((HD + 16, lanes), F32)
    for part, value in zip(parts, values):
        weights = jnp.exp2(part * factor - shift).astype(BF16)
        total = total + jnp.dot(value, weights, preferred_element_type=F32)
    peak, denom = top * scale, total[HD : HD + 1]
    mean = (total[0:HD] / denom).T.astype(BF16)
    totals = jnp.concatenate(
        [*in_three(peak), *in_three(denom), jnp.zeros((10, lanes), F32)], axis=0
    )
    for block in range(lanes // 64):
        at = slice(block * 64, (block + 1) * 64)
        out_ref[block, 0:64, :] = mean[at, :]
        out_ref[block, 64:80, :] = jnp.concatenate(
            [totals[:, at], totals[:, at]], axis=1
        ).astype(BF16)


def attend(queries, kv, values_t, fresh):
    step = 256
    rows = queries.shape[0]
    arrays = (kv, values_t, *fresh)

    def whole(array):
        return pl.BlockSpec(array.shape, lambda s: (0,) * array.ndim)

    return pl.pallas_call(
        attend_kernel,
        grid=(rows // step,),
        in_specs=[
            pl.BlockSpec((step, HD), lambda s: (s, 0)),
            *[whole(array) for array in arrays],
        ],
        out_specs=pl.BlockSpec((step // 64, 80, HD), lambda s: (s, 0, 0)),
        out_shape=jax.ShapeDtypeStruct((rows // 64, 80, HD), BF16),
        scratch_shapes=[pltpu.VMEM((2, HD + 16, 160), BF16)],
        compiler_params=pltpu.CompilerParams(vmem_limit_bytes=VMEM_LIMIT),
        cost_estimate=pl.CostEstimate(
            flops=4 * rows * 2368 * HD,
            bytes_accessed=3 * 2**20,
            transcendentals=rows * 2368,
        ),
    )(queries, *arrays)


def combine(in_ref):
    totals = in_ref[:, 64:80, :].astype(F32)
    peak = totals[:, 0, :] + totals[:, 1, :] + totals[:, 2, :]
    denom = totals[:, 3, :] + totals[:, 4, :] + totals[:, 5, :]
    even = lax.broadcasted_iota(jnp.int32, peak.shape, 0) % 2 == 0
    low = jnp.max(jnp.where(even, peak, -jnp.inf), axis=0, keepdims=True)
    high = jnp.max(jnp.where(even, -jnp.inf, peak), axis=0, keepdims=True)
    share = denom * jnp.exp(peak - jnp.where(even, low, high))
    low = jnp.sum(jnp.where(even, share, 0.0), axis=0, keepdims=True)
    high = jnp.sum(jnp.where(even, 0.0, share), axis=0, keepdims=True)
    share = (share / jnp.where(even, low, high)).T
    for xl in range(2):
        mixed = jnp.zeros((64, HD), F32)
        for i in range(xl, in_ref.shape[0], 2):
            mixed = mixed + in_ref[i, 0:64, :].astype(F32) * share[0:64, i : i + 1]
        yield mixed.astype(BF16)


def output_kernel(in_ref, w_ref, out_ref, att):
    @pl.when(pl.program_id(0) == 0)
    def _():
        for xl, rows in enumerate(combine(in_ref)):
            att[64 * xl : 64 * (xl + 1)] = rows

    attention = att[...]
    for m in range(8):
        weights = w_ref[2 * m : 2 * m + 2].reshape(320, HD)
        part = lax.dot_general(
            attention, weights, (((1,), (1,)), ((), ())), preferred_element_type=F32
        ).astype(BF16)
        for xl in range(2):
            block, at = part[64 * xl : 64 * (xl + 1)], 2 * (m // 2) + xl
            out_ref[m % 2, at, 0:64] = block[:, 0:HD]
            out_ref[m % 2, at, 64:128] = block[:, HD : 2 * HD]
            out_ref[m % 2, at, 128:160] = jnp.concatenate(
                [block[0:32, 2 * HD :], block[32:64, 2 * HD :]], axis=1
            )


def output_projection(shares, weights):
    return pl.pallas_call(
        output_kernel,
        grid=(2,),
        in_specs=[
            pl.BlockSpec(shares.shape, lambda s: (0, 0, 0)),
            pl.BlockSpec((16, 160, HD), lambda s: (0, s, 3)),
        ],
        out_specs=pl.BlockSpec((2, 8, 160, HD), lambda s: (0, s, 0, 0)),
        out_shape=jax.ShapeDtypeStruct((2, 16, 160, HD), BF16),
        scratch_shapes=[pltpu.VMEM((HD, HD), BF16)],
        compiler_params=pltpu.CompilerParams(vmem_limit_bytes=VMEM_LIMIT),
    )(shares, weights)


def over_heads_kernel(in_ref, y_ref, square_ref):
    total = in_ref[0].astype(F32)
    for i in range(1, in_ref.shape[0]):
        total = total + in_ref[i].astype(F32)
    last = jnp.concatenate([total[128:160, 0:64], total[128:160, 64:128]], axis=0)
    y = jnp.concatenate([total[0:64], total[64:128], last], axis=1)
    y_ref[...] = y
    squares = jnp.sum((y * y).T, axis=0, keepdims=True)
    for i in range(16):
        square_ref[i] = squares


def over_heads(parts):
    return pl.pallas_call(
        over_heads_kernel,
        out_shape=(
            jax.ShapeDtypeStruct((64, 320), F32),
            jax.ShapeDtypeStruct((16, 1, 64), F32),
        ),
        compiler_params=pltpu.CompilerParams(vmem_limit_bytes=VMEM_LIMIT),
    )(parts)


def from_neighbour(array):
    return lax.ppermute(array, "z", [(z, z ^ 1) for z in range(16)])


def local(
    state,
    clean_tokens,
    w_query,
    w_key,
    w_value,
    w_out,
    cache_keys,
    cache_values,
    norm_gain,
    mod_gain,
    out_gain,
    levels,
    noise_index,
    placement,
    group_mask,
):
    flight, ch_dev, width = state.shape
    rows_count = flight * ch_dev

    side = lax.axis_index("xl")
    tokens, shard = prepare(cache_keys, cache_values, w_key, w_value, w_query, w_out.T)
    near = from_neighbour(tokens)
    shard = swapped(shard, "xl")
    shard, near = lax.optimization_barrier((shard, near))
    w_full = lax.all_gather(shard.reshape(320, 4 * HD), "z", axis=0, tiled=False)

    current = level_lookup(levels, noise_index)
    following = level_lookup(levels, noise_index + 1)
    rows = jnp.concatenate(
        [state.reshape(rows_count, width), clean_tokens.astype(F32)], axis=0
    )
    sigma_rows = jnp.concatenate(
        [jnp.repeat(current, ch_dev), jnp.zeros((ch_dev,), F32)]
    )
    squares = sent_to_all(jnp.sum(rows * rows, axis=1), WIDE).sum(axis=0)
    inverse = lax.rsqrt(squares / D + EPSILON)
    features = (
        rows
        * inverse[:, None]
        * norm_gain[None, :]
        * (1.0 + sigma_rows[:, None] * mod_gain[None, :])
    ).astype(BF16)
    features = sent_to_all(features, ("y", "xh", "xl"))
    features = sent_to_all(features, "core").reshape(2, 4, 2, 2, 80, width)
    features = lay_out(features)

    table = jnp.arange(group_mask.shape[1], dtype=jnp.int32)
    held = (placement[:, None] == table[None, :]).astype(jnp.int32)
    seen = jnp.sum(held[None, :, :] * group_mask[:, None, :], axis=2) != 0
    seen = jnp.repeat(seen.T.astype(BF16), ch_dev, axis=1)
    seen = jnp.pad(jnp.concatenate([seen, seen], axis=1), ((0, 14), (0, 0)))
    kv = jnp.concatenate(
        [
            by_head(tokens),
            jnp.broadcast_to(seen[None], (2, *seen.shape)),
            by_head(near),
            jnp.broadcast_to(from_neighbour(seen)[None], (2, *seen.shape)),
        ],
        axis=1,
    )
    kv = swapped(kv, "xl").reshape(2, 2, 1040, HD)
    values_t = turn(kv)

    w_full, values_t, features = lax.optimization_barrier((w_full, values_t, features))
    queries = project(features, w_full, 2, HD, (16, 64, HD))
    queries = swapped(queries, "z").reshape(-1, HD)
    new = project(features, w_full, 0, 2 * HD, (320, HD))
    fresh = (new, from_neighbour(new))
    parts = attend(queries, kv, values_t, fresh)
    parts = swapped(parts, "z")
    parts = swapped(output_projection(parts, w_full), "core")
    parts = swapped(parts[0] + parts[1], ("y", "xh", "xl"))

    finished = new.reshape(2, 2, 80, HD)[:, :, 64:]
    mine = jnp.where(side == 0, finished[:, 0], finished[:, 1])
    other = jnp.where(side == 0, finished[:, 1], finished[:, 0])
    other = lax.ppermute(other, "xl", [(0, 1), (1, 0)])
    finished = jnp.where(
        side == 0,
        jnp.concatenate([mine, other], axis=2),
        jnp.concatenate([other, mine], axis=2),
    )
    new_keys, new_values = finished[0], finished[1]

    y, y_squares = over_heads(parts)
    y_squares = swapped(y_squares, WIDE).sum(axis=(0, 1))
    velocity = y * lax.rsqrt(y_squares / D + EPSILON)[:, None] * out_gain[None, :]
    step = jnp.repeat(following - current, ch_dev)[:, None]
    new_state = state.reshape(rows_count, width) + step * velocity
    new_state = new_state.reshape(flight, ch_dev, width)
    return new_state, new_keys, new_values


def solution(mesh):
    fine = Mesh(mesh.devices.reshape(4, 2, 16, 2, 2), ("y", "xl", "z", "xh", "core"))
    in_specs = (
        P(None, CTX, WIDE),
        P(CTX, WIDE),
        P(CTX, WIDE),
        P(CTX, WIDE),
        P(CTX, WIDE),
        P(WIDE, CTX),
        P(CTX, WIDE),
        P(CTX, WIDE),
        P(WIDE),
        P(WIDE),
        P(WIDE),
        P(),
        P(),
        P(CTX),
        P(),
    )
    out_specs = (P(None, CTX, WIDE), P(CTX, WIDE), P(CTX, WIDE))
    return jax.shard_map(local, mesh=fine, in_specs=in_specs, out_specs=out_specs, check_vma=False)
```

```python
import functools
import math

import jax
import jax.numpy as jnp
from jax import lax
from jax.experimental import pallas as pl
from jax.experimental.pallas import tpu as pltpu
from jax.sharding import Mesh
from jax.sharding import PartitionSpec as P

D = 5120
HD = 128
SLOT = 256
EPSILON = 1e-06
VMEM_LIMIT = 56 * 1024 * 1024

CTX = ("xl", "z")
WIDE = ("y", "xh", "core")
BF16 = jnp.bfloat16
F32 = jnp.float32


def level_lookup(levels, indices):
    table = jnp.arange(levels.shape[0], dtype=jnp.int32)
    picked = (indices[:, None] == table[None, :]).astype(F32)
    return jnp.sum(picked * levels[None, :], axis=1)


def sent_to_all(array, axis):
    devices = lax.axis_size(axis)
    return lax.all_to_all(
        jnp.broadcast_to(array[None], (devices, *array.shape)), axis, 0, 0, tiled=True
    )


def swapped(blocks, axis):
    return lax.all_to_all(blocks, axis, 0, 0, tiled=True)


def by_head(matrix):
    return jnp.stack([matrix[:, :HD], matrix[:, HD:]])


def prepare_kernel(keys_ref, values_ref, k_ref, v_ref, q_ref, out_ref, tokens_ref, shard_ref):
    tokens_ref[0:512, :] = keys_ref[...]
    tokens_ref[512:1024, :] = values_ref[...]
    for head in range(2):
        at = slice(HD * head, HD * (head + 1))
        for i, ref in enumerate((k_ref, v_ref, q_ref, out_ref)):
            shard_ref[head, :, HD * i : HD * (i + 1)] = ref[:, at]


def prepare(*arrays):
    return pl.pallas_call(
        prepare_kernel,
        out_shape=(
            jax.ShapeDtypeStruct((1024, 2 * HD), BF16),
            jax.ShapeDtypeStruct((2, 160, 4 * HD), BF16),
        ),
        compiler_params=pltpu.CompilerParams(vmem_limit_bytes=VMEM_LIMIT),
        cost_estimate=pl.CostEstimate(flops=0, bytes_accessed=2 * 2**20, transcendentals=0),
    )(*arrays)


def lay_out_kernel(h_ref, out_ref):
    for j in range(16):
        for xl in range(2):
            rows = h_ref[j % 2, j // 4, j // 2 % 2, xl]
            out_ref[80 * xl : 80 * (xl + 1), 320 * j : 320 * (j + 1)] = rows


def lay_out(features):
    return pl.pallas_call(
        lay_out_kernel,
        out_shape=jax.ShapeDtypeStruct((160, D), BF16),
        compiler_params=pltpu.CompilerParams(vmem_limit_bytes=VMEM_LIMIT),
        cost_estimate=pl.CostEstimate(flops=0, bytes_accessed=4 * 2**20, transcendentals=0),
    )(features)


def project_kernel(h_ref, w_ref, out_ref, acc):
    step = pl.program_id(0)
    width = acc.shape[1]
    weights = w_ref[...].reshape(D // 2, width)
    part = jnp.dot(h_ref[...], weights, preferred_element_type=F32)

    @pl.when(step == 0)
    def _():
        acc[...] = part

    @pl.when(step > 0)
    def _():
        acc[...] += part

    @pl.when(step == pl.num_programs(0) - 1)
    def _():
        total = acc[...]
        if width == HD:
            for xl in range(2):
                rows = total[80 * xl : 80 * xl + 64].astype(BF16)
                for i in range(8):
                    out_ref[2 * i + xl] = rows
        else:
            out_ref[0:160, :] = total[:, 0:HD].astype(BF16)
            out_ref[160:320, :] = total[:, HD:].astype(BF16)


def project(features, weights, block, width, shape):
    return pl.pallas_call(
        project_kernel,
        grid=(2,),
        in_specs=[
            pl.BlockSpec((160, D // 2), lambda s: (0, s)),
            pl.BlockSpec((16, 160, width), lambda s: (0, s, block)),
        ],
        out_specs=pl.BlockSpec(shape, lambda s: (0,) * len(shape)),
        out_shape=jax.ShapeDtypeStruct(shape, BF16),
        scratch_shapes=[pltpu.VMEM((160, width), F32)],
        compiler_params=pltpu.CompilerParams(vmem_limit_bytes=VMEM_LIMIT),
        cost_estimate=pl.CostEstimate(
            flops=2 * 160 * D * width, bytes_accessed=4 * 2**20, transcendentals=0
        ),
    )(features, weights)


def in_three(value):
    high = value.astype(BF16).astype(F32)
    middle = (value - high).astype(BF16).astype(F32)
    return [high, middle, value - high - middle]


def turn_kernel(kv_ref, out_ref):
    ones = (lax.broadcasted_iota(jnp.int32, (16, 512), 0) == 0).astype(F32).astype(BF16)
    for i in range(2):
        for side in range(2):
            values = kv_ref[side, i, 512:1024, :].astype(F32)
            out_ref[i, side, 0:HD] = values.T.astype(BF16)
            out_ref[i, side, HD : HD + 16] = ones


def turn(kv):
    return pl.pallas_call(
        turn_kernel,
        out_shape=jax.ShapeDtypeStruct((2, 2, HD + 16, 512), BF16),
        compiler_params=pltpu.CompilerParams(vmem_limit_bytes=VMEM_LIMIT),
        cost_estimate=pl.CostEstimate(flops=0, bytes_accessed=2**20, transcendentals=0),
    )(kv)


def attend_kernel(q_ref, kv_ref, vt_ref, own_new, other_new, out_ref, fresh_vt):
    @pl.when(pl.program_id(0) == 0)
    def _():
        ones = (lax.broadcasted_iota(jnp.int32, (16, 160), 0) == 0).astype(F32)
        for i, new in enumerate((own_new, other_new)):
            fresh_vt[i, 0:HD] = new[160:320, :].astype(F32).T.astype(BF16)
            fresh_vt[i, HD : HD + 16] = ones.astype(BF16)

    scale = 1.0 / math.sqrt(HD)
    queries = q_ref[...]
    lanes = queries.shape[0]
    across = (((1,), (1,)), ((), ()))

    def products(keys):
        return lax.dot_general(keys, queries, across, preferred_element_type=F32)

    token = lax.broadcasted_iota(jnp.int32, (160, lanes), 0)
    lane = lax.broadcasted_iota(jnp.int32, (160, lanes), 1)
    token = jnp.where(token >= 80, token - 80, token)
    visible = (token >= 64) | ((token >> 4) <= ((lane & 63) >> 4))

    parts, values = [], []
    for i, new in enumerate((own_new, other_new)):
        for side in range(2):
            seen = kv_ref[side, i, 1024:1040, :].astype(F32)
            hidden = jnp.where(seen > 0.5, 0.0, -jnp.inf)
            hidden = jnp.concatenate([hidden] * (lanes // HD), axis=1)
            for slot in range(2):
                at = slice(slot * SLOT, (slot + 1) * SLOT)
                parts.append(products(kv_ref[side, i, at, :]) + hidden[slot : slot + 1, :])
                values.append(vt_ref[i, side, :, at])
        parts.append(jnp.where(visible, products(new[0:160, :]), -jnp.inf))
        values.append(fresh_vt[i])

    top = functools.reduce(
        jnp.maximum, [jnp.max(part, axis=0, keepdims=True) for part in parts]
    )
    factor = scale * math.log2(math.e)
    shift = top * factor
    total = jnp.zeros((HD + 16, lanes), F32)
    for part, value in zip(parts, values):
        weights = jnp.exp2(part * factor - shift).astype(BF16)
        total = total + jnp.dot(value, weights, preferred_element_type=F32)
    peak, denom = top * scale, total[HD : HD + 1]
    mean = (total[0:HD] / denom).T.astype(BF16)
    totals = jnp.concatenate(
        [*in_three(peak), *in_three(denom), jnp.zeros((10, lanes), F32)], axis=0
    )
    for block in range(lanes // 64):
        at = slice(block * 64, (block + 1) * 64)
        out_ref[block, 0:64, :] = mean[at, :]
        out_ref[block, 64:80, :] = jnp.concatenate(
            [totals[:, at], totals[:, at]], axis=1
        ).astype(BF16)


def attend(queries, kv, values_t, fresh):
    step = 512
    rows = queries.shape[0]
    arrays = (kv, values_t, *fresh)

    def whole(array):
        return pl.BlockSpec(array.shape, lambda s: (0,) * array.ndim)

    return pl.pallas_call(
        attend_kernel,
        grid=(rows // step,),
        in_specs=[
            pl.BlockSpec((step, HD), lambda s: (s, 0)),
            *[whole(array) for array in arrays],
        ],
        out_specs=pl.BlockSpec((step // 64, 80, HD), lambda s: (s, 0, 0)),
        out_shape=jax.ShapeDtypeStruct((rows // 64, 80, HD), BF16),
        scratch_shapes=[pltpu.VMEM((2, HD + 16, 160), BF16)],
        compiler_params=pltpu.CompilerParams(vmem_limit_bytes=VMEM_LIMIT),
        cost_estimate=pl.CostEstimate(
            flops=4 * rows * 2368 * HD,
            bytes_accessed=3 * 2**20,
            transcendentals=rows * 2368,
        ),
    )(queries, *arrays)


def combine(in_ref):
    totals = in_ref[:, 64:80, :].astype(F32)
    peak = totals[:, 0, :] + totals[:, 1, :] + totals[:, 2, :]
    denom = totals[:, 3, :] + totals[:, 4, :] + totals[:, 5, :]
    even = lax.broadcasted_iota(jnp.int32, peak.shape, 0) % 2 == 0
    low = jnp.max(jnp.where(even, peak, -jnp.inf), axis=0, keepdims=True)
    high = jnp.max(jnp.where(even, -jnp.inf, peak), axis=0, keepdims=True)
    share = denom * jnp.exp(peak - jnp.where(even, low, high))
    low = jnp.sum(jnp.where(even, share, 0.0), axis=0, keepdims=True)
    high = jnp.sum(jnp.where(even, 0.0, share), axis=0, keepdims=True)
    share = (share / jnp.where(even, low, high)).T
    for xl in range(2):
        mixed = jnp.zeros((64, HD), F32)
        for i in range(xl, in_ref.shape[0], 2):
            mixed = mixed + in_ref[i, 0:64, :].astype(F32) * share[0:64, i : i + 1]
        yield mixed.astype(BF16)


def output_kernel(in_ref, w_ref, out_ref, att):
    @pl.when(pl.program_id(0) == 0)
    def _():
        for xl, rows in enumerate(combine(in_ref)):
            att[64 * xl : 64 * (xl + 1)] = rows

    attention = att[...]
    for m in range(8):
        weights = w_ref[2 * m : 2 * m + 2].reshape(320, HD)
        part = lax.dot_general(
            attention, weights, (((1,), (1,)), ((), ())), preferred_element_type=F32
        ).astype(BF16)
        for xl in range(2):
            block, at = part[64 * xl : 64 * (xl + 1)], 2 * (m // 2) + xl
            out_ref[m % 2, at, 0:64] = block[:, 0:HD]
            out_ref[m % 2, at, 64:128] = block[:, HD : 2 * HD]
            out_ref[m % 2, at, 128:160] = jnp.concatenate(
                [block[0:32, 2 * HD :], block[32:64, 2 * HD :]], axis=1
            )


def output_projection(shares, weights):
    return pl.pallas_call(
        output_kernel,
        grid=(2,),
        in_specs=[
            pl.BlockSpec(shares.shape, lambda s: (0, 0, 0)),
            pl.BlockSpec((16, 160, HD), lambda s: (0, s, 3)),
        ],
        out_specs=pl.BlockSpec((2, 8, 160, HD), lambda s: (0, s, 0, 0)),
        out_shape=jax.ShapeDtypeStruct((2, 16, 160, HD), BF16),
        scratch_shapes=[pltpu.VMEM((HD, HD), BF16)],
        compiler_params=pltpu.CompilerParams(vmem_limit_bytes=VMEM_LIMIT),
    )(shares, weights)


def over_heads_kernel(in_ref, y_ref, square_ref):
    total = in_ref[0].astype(F32)
    for i in range(1, in_ref.shape[0]):
        total = total + in_ref[i].astype(F32)
    last = jnp.concatenate([total[128:160, 0:64], total[128:160, 64:128]], axis=0)
    y = jnp.concatenate([total[0:64], total[64:128], last], axis=1)
    y_ref[...] = y
    squares = jnp.sum((y * y).T, axis=0, keepdims=True)
    for i in range(16):
        square_ref[i] = squares


def over_heads(parts):
    return pl.pallas_call(
        over_heads_kernel,
        out_shape=(
            jax.ShapeDtypeStruct((64, 320), F32),
            jax.ShapeDtypeStruct((16, 1, 64), F32),
        ),
        compiler_params=pltpu.CompilerParams(vmem_limit_bytes=VMEM_LIMIT),
    )(parts)


def from_neighbour(array):
    return lax.ppermute(array, "z", [(z, z ^ 1) for z in range(16)])


def local(
    state,
    clean_tokens,
    w_query,
    w_key,
    w_value,
    w_out,
    cache_keys,
    cache_values,
    norm_gain,
    mod_gain,
    out_gain,
    levels,
    noise_index,
    placement,
    group_mask,
):
    flight, ch_dev, width = state.shape
    rows_count = flight * ch_dev

    side = lax.axis_index("xl")
    tokens, shard = prepare(cache_keys, cache_values, w_key, w_value, w_query, w_out.T)
    near = from_neighbour(tokens)
    shard = swapped(shard, "xl")
    shard, near = lax.optimization_barrier((shard, near))
    w_full = lax.all_gather(shard.reshape(320, 4 * HD), "z", axis=0, tiled=False)

    current = level_lookup(levels, noise_index)
    following = level_lookup(levels, noise_index + 1)
    rows = jnp.concatenate(
        [state.reshape(rows_count, width), clean_tokens.astype(F32)], axis=0
    )
    sigma_rows = jnp.concatenate(
        [jnp.repeat(current, ch_dev), jnp.zeros((ch_dev,), F32)]
    )
    squares = sent_to_all(jnp.sum(rows * rows, axis=1), WIDE).sum(axis=0)
    inverse = lax.rsqrt(squares / D + EPSILON)
    features = (
        rows
        * inverse[:, None]
        * norm_gain[None, :]
        * (1.0 + sigma_rows[:, None] * mod_gain[None, :])
    ).astype(BF16)
    features = sent_to_all(features, ("y", "xh", "xl"))
    features = sent_to_all(features, "core").reshape(2, 4, 2, 2, 80, width)
    features = lay_out(features)

    table = jnp.arange(group_mask.shape[1], dtype=jnp.int32)
    held = (placement[:, None] == table[None, :]).astype(jnp.int32)
    seen = jnp.sum(held[None, :, :] * group_mask[:, None, :], axis=2) != 0
    seen = jnp.repeat(seen.T.astype(BF16), ch_dev, axis=1)
    seen = jnp.pad(jnp.concatenate([seen, seen], axis=1), ((0, 14), (0, 0)))
    kv = jnp.concatenate(
        [
            by_head(tokens),
            jnp.broadcast_to(seen[None], (2, *seen.shape)),
            by_head(near),
            jnp.broadcast_to(from_neighbour(seen)[None], (2, *seen.shape)),
        ],
        axis=1,
    )
    kv = swapped(kv, "xl").reshape(2, 2, 1040, HD)
    values_t = turn(kv)

    w_full, values_t, features = lax.optimization_barrier((w_full, values_t, features))
    queries = project(features, w_full, 2, HD, (16, 64, HD))
    queries = swapped(queries, "z").reshape(-1, HD)
    new = project(features, w_full, 0, 2 * HD, (320, HD))
    fresh = (new, from_neighbour(new))
    parts = attend(queries, kv, values_t, fresh)
    parts = swapped(parts, "z")
    parts = swapped(output_projection(parts, w_full), "core")
    parts = swapped(parts[0] + parts[1], ("y", "xh", "xl"))

    finished = new.reshape(2, 2, 80, HD)[:, :, 64:]
    mine = jnp.where(side == 0, finished[:, 0], finished[:, 1])
    other = jnp.where(side == 0, finished[:, 1], finished[:, 0])
    other = lax.ppermute(other, "xl", [(0, 1), (1, 0)])
    finished = jnp.where(
        side == 0,
        jnp.concatenate([mine, other], axis=2),
        jnp.concatenate([other, mine], axis=2),
    )
    new_keys, new_values = finished[0], finished[1]

    y, y_squares = over_heads(parts)
    y_squares = swapped(y_squares, WIDE).sum(axis=(0, 1))
    velocity = y * lax.rsqrt(y_squares / D + EPSILON)[:, None] * out_gain[None, :]
    step = jnp.repeat(following - current, ch_dev)[:, None]
    new_state = state.reshape(rows_count, width) + step * velocity
    new_state = new_state.reshape(flight, ch_dev, width)
    return new_state, new_keys, new_values


def solution(mesh):
    fine = Mesh(mesh.devices.reshape(4, 2, 16, 2, 2), ("y", "xl", "z", "xh", "core"))
    in_specs = (
        P(None, CTX, WIDE),
        P(CTX, WIDE),
        P(CTX, WIDE),
        P(CTX, WIDE),
        P(CTX, WIDE),
        P(WIDE, CTX),
        P(CTX, WIDE),
        P(CTX, WIDE),
        P(WIDE),
        P(WIDE),
        P(WIDE),
        P(),
        P(),
        P(CTX),
        P(),
    )
    out_specs = (P(None, CTX, WIDE), P(CTX, WIDE), P(CTX, WIDE))
    return jax.shard_map(local, mesh=fine, in_specs=in_specs, out_specs=out_specs, check_vma=False)
```
